256 devices in a mesh: section: 8 (over z), seq: 16 (over y, x), head: 2 (over core).
Axes of the slice: x: 4, y: 4, z: 8, core: 2. Of those that a mesh axis runs over, the one named last changes fastest.
Arguments:
- features: bfloat16 [8, 2048, 128, 64], P('section', 'seq', 'head'), may hold values from -1.1953125 to 1.1953125
- step_size: float32 [8, 2048, 128], P('section', 'seq', 'head'), may hold values from 0.5 to 2
- log_decay: float32 [8, 2048, 128], P('section', 'seq', 'head'), may hold values from -3 to 0
- input_map: bfloat16 [8, 2048, 4, 256], P('section', 'seq', 'head'), may hold values from -0.375 to 0.375
- output_map: bfloat16 [8, 2048, 4, 256], P('section', 'seq', 'head'), may hold values from -0.375 to 0.375
- segment: int32 [8, 2048], P('section', 'seq'), may hold values from 0 to 7, never falling along the last dimension, each value on 1 to 1024 neighbouring positions
- sent_grad: bfloat16 [8, 2048, 8192], P('section', ('seq', 'head')), may hold values from -3 to 3
Outputs:
- grad_features: bfloat16 [8, 2048, 128, 64], P('section', 'seq', 'head')
- grad_step: float32 [8, 2048, 128], P('section', 'seq', 'head')
- grad_decay: float32 [8, 2048, 128], P('section', 'seq', 'head')
- grad_input_map: float32 [8, 2048, 4, 256], P('section', 'seq', 'head')
- grad_output_map: float32 [8, 2048, 4, 256], P('section', 'seq', 'head')
The draws below stay inside these ranges and needn't reach their ends.
Inputs may be any that keep to these rules, and one draw needn't show every extreme that they name: `segment`: along each section's row the document numbers never fall; a document holds at most 1024 tokens, and one holds exactly that many.
All inputs are finite; a program needn't handle non-finite values.
Results may differ from the reference program's by a relative error of at most 0.039.
Values may be sent and summed in bfloat16 or wider, within the bound.
A program may use at most 192 MiB of HBM per device.

```python
import math
import jax
import jax.numpy as jnp
import numpy as np
from jax import lax

HEADS = 128
HEAD_DIM = 64
STATE = 256
GROUPS = 4
TOK_DEV = 128
DOCS = 8
RELAY_SECTIONS = 8
PACKED_TOKENS = 2048
N_SEQ = 16


def draw_log_decay(key, part):
    key = jax.random.fold_in(key, 11)
    random_keys = jax.random.split(key, 7)
    slow_share = 0.5
    slow = jax.random.uniform(random_keys[0], (RELAY_SECTIONS, 1, HEADS)) < slow_share
    slow_rate = jnp.exp(jax.random.uniform(random_keys[1], (RELAY_SECTIONS, 1, HEADS), minval=jnp.log(0.1), maxval=jnp.log(0.5))) / PACKED_TOKENS
    fast_rate = jnp.exp(jax.random.uniform(random_keys[2], (RELAY_SECTIONS, 1, HEADS), minval=jnp.log(1.0 / 50.0), maxval=jnp.log(1.0 / 30.0)))
    decay_speed = jnp.where(slow, slow_rate, fast_rate)
    random_noise = jnp.exp(jax.random.uniform(random_keys[3], (RELAY_SECTIONS, PACKED_TOKENS, HEADS), minval=-0.69, maxval=0.69))
    blocks = PACKED_TOKENS // TOK_DEV
    block_scale_factor = jnp.exp(jax.random.uniform(random_keys[4], (RELAY_SECTIONS, blocks, 1, HEADS), minval=-0.69, maxval=0.69))
    block_scale_factor = jnp.broadcast_to(block_scale_factor, (RELAY_SECTIONS, blocks, TOK_DEV, HEADS)).reshape(RELAY_SECTIONS, PACKED_TOKENS, HEADS)
    spike_location = jax.random.randint(random_keys[5], (RELAY_SECTIONS, 3, 1), 0, PACKED_TOKENS)
    spike_magnitude = jax.random.uniform(random_keys[6], (RELAY_SECTIONS, 3, 1), minval=0.22, maxval=0.69)
    token_positions = jnp.arange(PACKED_TOKENS)[None, None, :]
    spike_event = jnp.sum(jnp.where(token_positions == spike_location, spike_magnitude, 0.0), axis=1)
    return (-(decay_speed * random_noise * block_scale_factor) - spike_event[:, :, None]).astype(jnp.float32)


def steps_of(key, shape, cuts, smallest, top_value):
    level, own = 1.0, jax.random.fold_in(key, 6)
    for dim, shards_of in cuts:
        heights = jnp.exp(jax.random.uniform(jax.random.fold_in(own, dim), (shards_of,), jnp.float32, smallest / len(cuts), top_value / len(cuts)))
        level = level * jnp.repeat(heights, shape[dim] // shards_of).reshape([-1 if axis == dim else 1 for axis in range(len(shape))])
    return level


def profile(number_of, total, limit, skew):
    weights = [(1 << 20) // math.isqrt(standing ** skew) + 1 for standing in range(2, number_of + 1)]
    spare, given = total - limit - (number_of - 1), [1] * (number_of - 1)
    while spare > 0:
        free = [i for i in range(number_of - 1) if given[i] < limit]
        pool, remaining = sum([weights[i] for i in free]), spare
        for i in free:
            extra = min(limit - given[i], max(1, remaining * weights[i] // pool), spare)
            given[i] = given[i] + extra
            spare = spare - extra
    return np.array([limit] + given)


def uneven(rng, number_of, total, most, skew):
    if number_of == 2:
        one = jax.random.randint(rng, (), max(1, total - most), min(most, total - 1) + 1)
        return jnp.stack([one, total - one])
    sizes = jnp.asarray(profile(number_of, total, most, skew), jnp.int32)
    pairs = (number_of - 1) // 2
    donor, receiver = sizes[1:1 + 2 * pairs:2], sizes[2:2 + 2 * pairs:2]
    room = jnp.minimum(donor - 1, most - receiver)
    shifted = jax.random.randint(jax.random.fold_in(rng, 1), (pairs,), 0, 1 << 20) % (room + 1)
    sizes = sizes.at[1:1 + 2 * pairs:2].set(donor - shifted).at[2:2 + 2 * pairs:2].set(receiver + shifted)
    return sizes[jax.random.permutation(jax.random.fold_in(rng, 2), number_of)]


def centred(stream_key, dims, scale, reach, cuts=(), held_as=jnp.bfloat16):
    result = jax.random.normal(stream_key, dims, jnp.float32) * scale
    if len(cuts) > 0:
        result = steps_of(stream_key, dims, cuts, -0.22, 0.18) * result
    return jnp.clip(result, min=-reach, max=reach).astype(held_as)


def setup_inputs(seed: int = 0) -> dict:
    keys = jax.random.split(jax.random.key(seed), 8)
    features = centred(keys[0], (RELAY_SECTIONS, PACKED_TOKENS, HEADS, HEAD_DIM), 0.2, 1.1953125, ((0, 8), (1, 16), (2, 2)))
    step_size = jnp.clip(jnp.exp(math.log(2.0) - 1.3862944 * jax.random.uniform(keys[1], (RELAY_SECTIONS, PACKED_TOKENS, HEADS), jnp.float32) ** steps_of(keys[1], (RELAY_SECTIONS, PACKED_TOKENS, HEADS), ((0, 8), (1, 16), (2, 2)), -0.2, 0.2)), 0.5, 2.0)
    log_decay = draw_log_decay(jax.random.fold_in(keys[7], 71), 0)
    input_map = centred(keys[3], (RELAY_SECTIONS, PACKED_TOKENS, GROUPS, STATE), STATE ** -0.5, 0.375, ((0, 8), (1, 16), (2, 2)))
    output_map = centred(keys[4], (RELAY_SECTIONS, PACKED_TOKENS, GROUPS, STATE), STATE ** -0.5, 0.375, ((0, 8), (1, 16), (2, 2)))
    segment = jax.vmap(lambda own: jnp.searchsorted(jnp.cumsum(uneven(own, DOCS, PACKED_TOKENS, PACKED_TOKENS // 2, 2)), jnp.arange(PACKED_TOKENS), side="right"))(jax.random.split(keys[5], RELAY_SECTIONS)).reshape((RELAY_SECTIONS, PACKED_TOKENS)).astype(jnp.int32)
    sent_grad = centred(keys[6], (RELAY_SECTIONS, PACKED_TOKENS, HEADS * HEAD_DIM), 0.5, 3.0, ((0, 8), (1, 32)))
    return dict(features=features, step_size=step_size, log_decay=log_decay, input_map=input_map, output_map=output_map, segment=segment, sent_grad=sent_grad)


highest = lax.Precision.HIGHEST


def layout(features, step_size, log_decay, input_map, output_map, segments, previous):
    length, heads, width = features.shape
    repeat = heads // input_map.shape[1]
    feat32 = features.astype(jnp.float32)
    map_in = jnp.repeat(input_map.astype(jnp.float32), repeat, axis=1)
    map_out = jnp.repeat(output_map.astype(jnp.float32), repeat, axis=1)
    cumulative = jnp.cumsum(log_decay, axis=0)
    carried = (segments == previous).astype(jnp.float32)
    token_positions = jnp.arange(length, dtype=jnp.int32)
    same_doc = (segments[:, None] == segments[None, :]) & (token_positions[:, None] >= token_positions[None, :])
    along = cumulative.T
    log_gaps = along[:, :, None] - along[:, None, :]
    forward_mask = jnp.where(same_doc[None], jnp.exp(jnp.where(same_doc[None], log_gaps, 0.0)), 0.0)
    head_weight = carried[:, None] * jnp.exp(cumulative)
    tail_mask = (segments == segments[-1]).astype(jnp.float32)
    tail_weight = tail_mask[:, None] * jnp.exp(cumulative[-1][None, :] - cumulative)
    decay_total = carried[-1] * jnp.exp(cumulative[-1])
    return (feat32, map_in, map_out, forward_mask, head_weight, tail_weight, decay_total)


def state_summary(parts, step_size):
    feat32, map_in, map_out, forward_mask, head_weight, tail_weight, decay_total = parts
    end_weight = forward_mask[:, -1, :].T * step_size
    return jnp.einsum('thn,thp->hnp', end_weight[:, :, None] * map_in, feat32, precision=highest)


def grad_summary(parts, grad32):
    feat32, map_in, map_out, forward_mask, head_weight, tail_weight, decay_total = parts
    return jnp.einsum('thn,thp->hnp', head_weight[:, :, None] * map_out, grad32, precision=highest)


def finish(parts, grad32, step_size, state_in, grad_in, groups):
    feat32, map_in, map_out, forward_mask, head_weight, tail_weight, decay_total = parts
    length, heads, width = feat32.shape
    depth = map_in.shape[2]
    backward_mask = jnp.swapaxes(forward_mask, 1, 2)
    cross = jnp.einsum('thn,rhn->htr', map_in, map_out, precision=highest)
    pairs = jnp.einsum('thp,shp->hts', grad32, feat32, precision=highest)
    lifted = jnp.einsum('thn,hnp->thp', map_in, grad_in, precision=highest)
    value = jnp.einsum('htr,rhp->thp', backward_mask * cross, grad32, precision=highest) + tail_weight[:, :, None] * lifted
    grad_features = (step_size[:, :, None] * value).astype(jnp.bfloat16)
    grad_step = jnp.sum(feat32 * value, axis=2)
    into_map = jnp.einsum('htr,rhn->thn', backward_mask * jnp.swapaxes(pairs, 1, 2), map_out, precision=highest)
    into_map = step_size[:, :, None] * (into_map + tail_weight[:, :, None] * jnp.einsum('thp,hnp->thn', feat32, grad_in, precision=highest))
    weighted = forward_mask * pairs * step_size.T[:, None, :]
    out_map = jnp.einsum('hts,shn->thn', weighted, map_in, precision=highest) + head_weight[:, :, None] * jnp.einsum('thp,hnp->thn', grad32, state_in, precision=highest)
    kernel = jnp.swapaxes(cross, 1, 2) * pairs * step_size.T[:, None, :]
    chained = jnp.einsum('htr,hrs->hts', backward_mask, kernel, precision=highest)
    first = jnp.sum(chained * forward_mask, axis=2).T
    seen = jnp.einsum('thn,hnp->thp', map_out, state_in, precision=highest)
    second = head_weight * jnp.einsum('htr,rh->th', backward_mask, jnp.sum(seen * grad32, axis=2), precision=highest)
    third = tail_weight * jnp.einsum('hts,sh->th', forward_mask, step_size * jnp.sum(lifted * feat32, axis=2), precision=highest)
    fourth = tail_weight * head_weight * jnp.sum(grad_in * state_in, axis=(1, 2))[None, :]
    grad_decay = first + second + third + fourth - step_size * grad_step
    repeat = heads // groups
    grad_in_map = into_map.reshape(length, groups, repeat, depth).sum(axis=2)
    grad_out_map = out_map.reshape(length, groups, repeat, depth).sum(axis=2)
    return grad_features, grad_step, grad_decay, grad_in_map, grad_out_map


def combine(earlier, later):
    decay_early = earlier[0].astype(jnp.float32)
    decay_late = later[0].astype(jnp.float32)
    state_early = earlier[1].astype(jnp.float32)
    state_late = later[1].astype(jnp.float32)
    joined = state_late + decay_late[:, None, None] * state_early
    return ((decay_early * decay_late).astype(jnp.bfloat16), joined.astype(jnp.bfloat16))


def reference(features, step_size, log_decay, input_map, output_map, segment, sent_grad):
    results = []
    for section_index in range(RELAY_SECTIONS):
        grads_all = sent_grad[(section_index + 1) % RELAY_SECTIONS].reshape(N_SEQ, TOK_DEV, HEADS, HEAD_DIM)
        feats = features[section_index].reshape(N_SEQ, TOK_DEV, HEADS, HEAD_DIM)
        steps_block = step_size[section_index].reshape(N_SEQ, TOK_DEV, HEADS)
        decays = log_decay[section_index].reshape(N_SEQ, TOK_DEV, HEADS)
        maps_in = input_map[section_index].reshape(N_SEQ, TOK_DEV, GROUPS, STATE)
        maps_out = output_map[section_index].reshape(N_SEQ, TOK_DEV, GROUPS, STATE)
        segs = segment[section_index].reshape(N_SEQ, TOK_DEV)
        previous = jnp.concatenate([jnp.zeros((1,), jnp.int32), segs[:-1, -1].astype(jnp.int32)])
        blocks = (feats, grads_all, steps_block, decays, maps_in, maps_out, segs, previous)

        def summarize(block):
            feat_block, grad_block, step_block, decay_block, in_block, out_block, seg_block, prev_block = block
            parts = layout(feat_block, step_block, decay_block, in_block, out_block, seg_block, prev_block)
            grad32 = grad_block.astype(jnp.float32)
            return (parts[6].astype(jnp.bfloat16), state_summary(parts, step_block).astype(jnp.bfloat16), grad_summary(parts, grad32).astype(jnp.bfloat16))

        decay_sums, state_sums, grad_sums = lax.map(summarize, blocks)
        identity = (jnp.ones((HEADS,), jnp.bfloat16), jnp.zeros((HEADS, STATE, HEAD_DIM), jnp.bfloat16))

        def carry_step(carry, item):
            return combine(carry, item), carry[1]

        unused_one, states_in = lax.scan(carry_step, identity, (decay_sums, state_sums))
        unused_two, grads_in = lax.scan(carry_step, identity, (decay_sums, grad_sums), reverse=True)

        def complete(block):
            feat_block, grad_block, step_block, decay_block, in_block, out_block, seg_block, prev_block, state_block, carry_block = block
            parts = layout(feat_block, step_block, decay_block, in_block, out_block, seg_block, prev_block)
            return finish(parts, grad_block.astype(jnp.float32), step_block, state_block.astype(jnp.float32), carry_block.astype(jnp.float32), GROUPS)

        outs = lax.map(complete, blocks + (states_in, grads_in))
        results.append((outs[0].reshape(PACKED_TOKENS, HEADS, HEAD_DIM), outs[1].reshape(PACKED_TOKENS, HEADS), outs[2].reshape(PACKED_TOKENS, HEADS), outs[3].reshape(PACKED_TOKENS, GROUPS, STATE), outs[4].reshape(PACKED_TOKENS, GROUPS, STATE)))
    return (jnp.stack([item[0] for item in results]), jnp.stack([item[1] for item in results]), jnp.stack([item[2] for item in results]), jnp.stack([item[3] for item in results]), jnp.stack([item[4] for item in results]))
```

```python
import jax
import jax.numpy as jnp
from jax import lax
from jax.experimental import pallas as pl
from jax.experimental.pallas import tpu as pltpu
from jax.sharding import PartitionSpec as P

MESH = pl.DeviceIdType.MESH
F32 = jnp.float32
BF16 = jnp.bfloat16
HIGHEST = lax.Precision.HIGHEST

T = 128
W = 64
N = 256
ROW = 4
HEADS = 16
CHUNKS = 4
HC = HEADS // CHUNKS
CW = HC * W


def dot(a, b, precision=None):
    return lax.dot_general(
        a, b, (((1,), (0,)), ((), ())), precision=precision, preferred_element_type=F32
    )


def dot_nt(a, b, precision=None):
    return lax.dot_general(
        a, b, (((1,), (1,)), ((), ())), precision=precision, preferred_element_type=F32
    )


def dot_tn(a, b):
    return lax.dot_general(a, b, (((0,), (0,)), ((), ())), preferred_element_type=F32)


def place(s, y, x, c):
    return {
        "section": lax.rem(s + 8, 8),
        "seq": lax.rem(y + 4, 4) * 4 + lax.rem(x + 4, 4),
        "head": lax.rem(c, 2),
    }


def kernel(
    feat, step, dec, maps, seg, grad,
    gf_out, gs_out, gd_out, gim_out, gom_out,
    XT, XW, GRN, GRT, GHW, MAP, STEP, DEC, SEG, PREV,
    L, LT, HW, TW, STW, DB, CF, CB, CM, MASK, PRE,
    PF, PB, VI, WS, CK, RK, U, V, B4,
    EB, GB, ES, GS, GIM, GOM, PMS, PM, GF, GSS, GDS,
    ssem, rs_one, rs_feat, rs_grad, rs_f, rs_b,
):
    s = lax.axis_index("section")
    q = lax.axis_index("seq")
    c = lax.axis_index("head")
    y = q // 4
    x = lax.rem(q, 4)
    gl_mine = lax.rem(x, 2)
    co = x // 2
    R_SEG, R_STEP, R_DEC, R_MAP, R_PREV, R_GF, R_GS, R_GD, R_PM = range(9)

    barrier = pltpu.get_barrier_semaphore()
    for dx in range(4):
        for dc in range(2):
            if dx or dc:
                pl.semaphore_signal(barrier, inc=1, device_id=place(s, y, x + dx, c + dc), device_id_type=MESH)
            pl.semaphore_signal(barrier, inc=1, device_id=place(s + 1, y, x + dx, c + dc), device_id_type=MESH)
    for dy in (1, -1):
        pl.semaphore_signal(barrier, inc=1, device_id=place(s, y + dy, x, c), device_id_type=MESH)
    pl.semaphore_wait(barrier, 17)

    pending = []

    def send(src, dst, rsem, target, own=None):
        copy = pltpu.make_async_remote_copy(
            src_ref=src, dst_ref=dst, send_sem=ssem.at[len(pending)], recv_sem=rsem,
            device_id=target, device_id_type=MESH,
        )
        if own is None:
            copy.start()
            pending.append((None, copy))
        else:
            away = jnp.logical_not(own)

            @pl.when(own)
            def _():
                pltpu.make_async_copy(src, dst, rsem).start()

            @pl.when(away)
            def _():
                copy.start()

            pending.append((away, copy))

    def arrived(ref, sem):
        pltpu.make_async_copy(ref, ref, sem).wait()

    pltpu.make_async_copy(seg, SEG.at[x], rs_one.at[R_SEG]).start()
    for dx in range(1, 4):
        send(seg, SEG.at[x], rs_one.at[R_SEG], place(s, y, x + dx, c))
    workers = []
    for gl in range(2):
        for dc in range(2):
            xw = 2 * c + gl
            cw = lax.rem(c + dc, 2)
            workers.append((gl, xw, cw, (xw == x) if dc == 0 else None))
    for gl, xw, cw, own in workers:
        rows = pl.ds(pl.multiple_of(32 * gl + 16 * cw, 16), 16)
        send(step.at[rows], STEP.at[x], rs_one.at[R_STEP], place(s, y, xw, cw), own)
        send(dec.at[rows], DEC.at[x], rs_one.at[R_DEC], place(s, y, xw, cw), own)
    for gl, xw, cw, own in workers:
        send(maps.at[gl], MAP.at[x], rs_one.at[R_MAP], place(s, y, xw, cw), own)
    for k in range(CHUNKS):
        for gl, xw, cw, own in workers:
            rows = pl.ds(pl.multiple_of((32 * gl + 16 * cw + HC * k) * W, CW), CW)
            send(feat.at[rows], XT.at[k, x], rs_feat.at[k], place(s, y, xw, cw), own)
        for dx in range(4):
            for dc in range(2):
                xw = lax.rem(x + dx, 4)
                cw = lax.rem(c + dc, 2)
                cols = pl.ds(pl.multiple_of((32 * xw + 16 * cw + HC * k) * W, CW), CW)
                send(
                    grad.at[:, cols],
                    GRN.at[k, x, pl.ds(pl.multiple_of(64 * c, 64), 64), :],
                    rs_grad.at[k],
                    place(s - 1, y, xw, cw),
                )

    arrived(SEG, rs_one.at[R_SEG])
    send(SEG.at[3], PREV, rs_one.at[R_PREV], place(s, y + 1, x, c))
    arrived(STEP, rs_one.at[R_STEP])
    arrived(DEC, rs_one.at[R_DEC])
    row_id = lax.broadcasted_iota(jnp.int32, (T, T), 0)
    col_id = lax.broadcasted_iota(jnp.int32, (T, T), 1)
    upper = (row_id <= col_id).astype(F32)
    for b in range(ROW):
        total = dot(DEC[b], upper, HIGHEST)
        L[b] = total
        padded = jnp.concatenate([total, jnp.zeros((T - HEADS, T), F32)], axis=0)
        LT[b] = jnp.transpose(padded)
        seg_row = SEG[b][0:1, :]
        seg_col = jnp.transpose(jnp.broadcast_to(seg_row, (T, T)))
        same = (seg_col == seg_row).astype(F32)
        MASK[b] = jnp.where(row_id >= col_id, same, 0.0)
        PRE[b] = jnp.where(row_id < col_id, same, 0.0)
    arrived(PREV, rs_one.at[R_PREV])
    first = (y > 0).astype(F32)
    decays = []
    for b in range(ROW):
        total = L[b]
        seg_row = SEG[b][0:1, :]
        if b == 0:
            previous = PREV[0:1, T - 1 : T] * first
        else:
            previous = SEG[b - 1][0:1, T - 1 : T]
        last = total[:, T - 1 : T]
        seg_last = seg_row[:, T - 1 : T]
        carried = (seg_row == previous).astype(F32)
        tail = (seg_row == seg_last).astype(F32)
        HW[b] = carried * jnp.exp(total)
        tw = tail * jnp.exp(last - total)
        TW[b] = tw
        STW[b] = STEP[b] * tw
        d = jnp.broadcast_to((seg_last == previous).astype(F32) * jnp.exp(last), (HEADS, N))
        DB[b] = d
        decays.append(d)
    one = jnp.ones((HEADS, N), F32)
    run = one
    for b in range(ROW):
        CF[b] = run
        run = run * decays[b]
    CF[ROW] = run
    run = one
    for b in reversed(range(ROW)):
        CB[b] = run
        run = run * decays[b]
    arrived(MAP, rs_one.at[R_MAP])
    for b in range(ROW):
        CM[b] = dot_nt(MAP[b, 1], MAP[b, 0])
        WS[b] = jnp.zeros((T, T), F32)
        RK[b] = jnp.zeros((T, T), F32)
        GIM[b] = jnp.zeros((T, N), F32)
        GOM[b] = jnp.zeros((T, N), F32)

    def by_head(a):
        return a.reshape(HC, W, a.shape[-1])

    def scaled(a, w):
        return (by_head(a) * w[:, None, :]).reshape(a.shape)

    def heads_of(ref, b, k):
        return ref[b, HC * k : HC * (k + 1), :]

    def local_states(k):
        arrived(XT.at[k], rs_feat.at[k])
        total = jnp.zeros((CW, N), F32)
        PF[k, 0] = total
        for b in range(ROW):
            xw = scaled(XT[k, b].astype(F32), heads_of(STW, b, k)).astype(BF16)
            XW[k, b] = xw
            total = scaled(total, heads_of(DB, b, k)) + dot(xw, MAP[b, 0])
            PF[k, b + 1] = total

    def local_grads(k):
        arrived(GRN.at[k], rs_grad.at[k])
        total = jnp.zeros((CW, N), F32)
        PB[k, ROW] = total
        for b in reversed(range(ROW)):
            gt = jnp.transpose(GRN[k, b])
            GRT[k, b] = gt
            gh = scaled(gt.astype(F32), heads_of(HW, b, k)).astype(BF16)
            GHW[k, b] = gh
            total = scaled(total, heads_of(DB, b, k)) + dot(gh, MAP[b, 1])
            PB[k, b] = total

    def take_f(k):
        @pl.when(y > 0)
        def _():
            arrived(EB.at[k], rs_f.at[k])

        @pl.when(y == 0)
        def _():
            EB[k] = jnp.zeros((CW, N), BF16)

    def take_b(k):
        @pl.when(y < 3)
        def _():
            arrived(GB.at[k], rs_b.at[k])

        @pl.when(y == 3)
        def _():
            GB[k] = jnp.zeros((CW, N), BF16)

    fsend = {}
    bsend = {}

    def forward_f(k):
        entering = scaled(EB[k].astype(F32), heads_of(CF, ROW, k))
        ES[k] = (entering + PF[k, ROW]).astype(BF16)
        fsend[k].start()

    def forward_b(k):
        whole = heads_of(CF, ROW, k)
        entering = scaled(GB[k].astype(F32), whole)
        GS[k] = (entering + PB[k, 0]).astype(BF16)
        bsend[k].start()

    def prepare(k):
        n = len(pending)
        fsend[k] = pltpu.make_async_remote_copy(
            src_ref=ES.at[k], dst_ref=EB.at[k], send_sem=ssem.at[n], recv_sem=rs_f.at[k],
            device_id=place(s, y + 1, x, c), device_id_type=MESH,
        )
        pending.append((y < 3, fsend[k]))
        bsend[k] = pltpu.make_async_remote_copy(
            src_ref=GS.at[k], dst_ref=GB.at[k], send_sem=ssem.at[n + 1], recv_sem=rs_b.at[k],
            device_id=place(s, y - 1, x, c), device_id_type=MESH,
        )
        pending.append((y > 0, bsend[k]))

    def hop_f(k, at):
        @pl.when(y == at)
        def _():
            take_f(k)
            forward_f(k)

    def hop_b(k, at):
        @pl.when(y == at)
        def _():
            take_b(k)
            forward_b(k)

    def intra(k):
        def one_block(b, carry):
            xt = XT[k, b]
            zero = jnp.zeros((W, T), BF16)
            spread = jnp.concatenate(
                [
                    jnp.concatenate(
                        [xt[W * h : W * (h + 1)] if h == j else zero for j in range(HC)], axis=1
                    )
                    for h in range(HC)
                ],
                axis=0,
            )
            pairs = dot(GRN[k, b], spread)
            mask = MASK[b] > 0.0
            cross = CM[b]
            columns = LT[b]
            held = WS[b]
            sums = RK[b]
            lane = lax.broadcasted_iota(jnp.int32, (T, T), 1)
            cols = []
            for h in range(HC):
                head = HC * k + h
                gap = columns[:, head : head + 1] - L[b, head : head + 1, :]
                m = jnp.where(mask, jnp.exp(gap), 0.0)
                a = (m * cross).astype(BF16)
                VI[k, b, W * h : W * (h + 1), :] = dot(GRT[k, b, W * h : W * (h + 1), :], a)
                wh = m * pairs[:, T * h : T * (h + 1)] * STEP[b, head : head + 1, :]
                held = held + wh
                kk = wh * cross
                cols.append(jnp.sum(kk, axis=0, keepdims=True))
                sums = jnp.where(lane == head, jnp.sum(kk, axis=1, keepdims=True), sums)
            CK[b, HC * k : HC * (k + 1), :] = jnp.concatenate(cols, axis=0)
            WS[b] = held
            RK[b] = sums
            return carry

        lax.fori_loop(0, ROW, one_block, 0)

    def finish(k):
        def one_block(b, carry):
            e = EB[k].astype(F32)
            g = GB[k].astype(F32)
            eb = (PF[k, b] + scaled(e, heads_of(CF, b, k))).astype(BF16)
            gb = (PB[k, b + 1] + scaled(g, heads_of(CB, b, k))).astype(BF16)
            lift = dot_nt(gb, MAP[b, 0])
            seen = dot_nt(eb, MAP[b, 1])
            val = VI[k, b] + scaled(lift, heads_of(TW, b, k))
            GF[k, b] = scaled(val, heads_of(STEP, b, k)).astype(BF16)
            hs = slice(HC * k, HC * (k + 1))
            V[b, hs, :] = heads_of(STW, b, k) * jnp.sum(by_head(XT[k, b].astype(F32) * lift), axis=1)
            U[b, hs, :] = heads_of(HW, b, k) * jnp.sum(by_head(GRT[k, b].astype(F32) * seen), axis=1)
            both = jnp.sum(by_head(eb.astype(F32) * gb.astype(F32)), axis=1)
            B4[b, hs, :] = jnp.broadcast_to(jnp.sum(both, axis=1, keepdims=True), (HC, T))
            GIM[b] += dot_tn(XW[k, b], gb)
            GOM[b] += dot_tn(GHW[k, b], eb)
            return carry

        lax.fori_loop(0, ROW, one_block, 0)
        for dx in range(4):
            xo = lax.rem(x + dx, 4)
            rows = pl.ds(pl.multiple_of((32 * gl_mine + 16 * c + HC * k) * W, CW), CW)
            send(
                GF.at[k, xo], gf_out.at[rows], rs_one.at[R_GF],
                place(s, y, xo, co), (c == co) if dx == 0 else None,
            )

    for k in range(CHUNKS):
        prepare(k)
    for k in range(CHUNKS + 2):
        if k < CHUNKS:
            local_states(k)
            hop_f(k, 0)
            local_grads(k)
            hop_b(k, 3)
            intra(k)
        if 0 <= k - 1 < CHUNKS:
            hop_b(k - 1, 1)
            hop_f(k - 1, 2)
        if k < CHUNKS:
            hop_f(k, 1)
            hop_b(k, 2)
        if 0 <= k - 2:
            @pl.when(y == 0)
            def _():
                take_b(k - 2)

            @pl.when(y == 3)
            def _():
                take_f(k - 2)

            finish(k - 2)

    for b in range(ROW):
        w = WS[b].astype(BF16)
        PMS[b, 0] = (GIM[b] + dot_tn(w, MAP[b, 1])).astype(BF16)
        PMS[b, 1] = (GOM[b] + dot(w, MAP[b, 0])).astype(BF16)
    for dx in range(4):
        xo = lax.rem(x + dx, 4)
        own = (c == co) if dx == 0 else None
        send(PMS.at[xo], PM.at[gl_mine, c], rs_one.at[R_PM], place(s, y, xo, co), own)
    for b in range(ROW):
        row_sums = jnp.transpose(RK[b])[0:HEADS, :]
        ck = CK[b]
        v = V[b]
        GSS[b] = (ck + v) / STEP[b]
        chain = dot(row_sums - ck + U[b], MASK[b], HIGHEST) + dot(v, PRE[b], HIGHEST)
        GDS[b] = chain + HW[b] * TW[b] * B4[b]
    for dx in range(4):
        xo = lax.rem(x + dx, 4)
        own = (c == co) if dx == 0 else None
        rows = pl.ds(pl.multiple_of(32 * gl_mine + 16 * c, 16), 16)
        send(GSS.at[xo], gs_out.at[rows], rs_one.at[R_GS], place(s, y, xo, co), own)
        send(GDS.at[xo], gd_out.at[rows], rs_one.at[R_GD], place(s, y, xo, co), own)

    arrived(PM, rs_one.at[R_PM])
    for gl in range(2):
        gim_out[gl] = PM[gl, 0, 0].astype(F32) + PM[gl, 1, 0].astype(F32)
        gom_out[gl] = PM[gl, 0, 1].astype(F32) + PM[gl, 1, 1].astype(F32)
    arrived(gf_out, rs_one.at[R_GF])
    arrived(gs_out, rs_one.at[R_GS])
    arrived(gd_out, rs_one.at[R_GD])
    for cond, copy in pending:
        if cond is None:
            copy.wait_send()
        else:
            @pl.when(cond)
            def _():
                copy.wait_send()


def per_device(features, step_size, log_decay, input_map, output_map, segment, sent_grad):
    feat = jnp.transpose(features[0], (1, 2, 0)).reshape(64 * W, T)
    step = step_size[0].T
    dec = log_decay[0].T
    maps = jnp.transpose(jnp.stack([input_map[0], output_map[0]]), (2, 0, 1, 3))
    seg = jnp.broadcast_to(segment.astype(F32), (8, T))
    grad = sent_grad[0]
    any_ = pl.BlockSpec(memory_space=pl.ANY)
    vmem = pl.BlockSpec(memory_space=pltpu.VMEM)
    V_ = pltpu.VMEM
    scratch = [
        V_((CHUNKS, ROW, CW, T), BF16),
        V_((CHUNKS, ROW, CW, T), BF16),
        V_((CHUNKS, ROW, T, CW), BF16),
        V_((CHUNKS, ROW, CW, T), BF16),
        V_((CHUNKS, ROW, CW, T), BF16),
        V_((ROW, 2, T, N), BF16),
        V_((ROW, HEADS, T), F32),
        V_((ROW, HEADS, T), F32),
        V_((ROW, 8, T), F32),
        V_((8, T), F32),
        V_((ROW, HEADS, T), F32),
        V_((ROW, T, T), F32),
        V_((ROW, HEADS, T), F32),
        V_((ROW, HEADS, T), F32),
        V_((ROW, HEADS, T), F32),
        V_((ROW, HEADS, N), F32),
        V_((ROW + 1, HEADS, N), F32),
        V_((ROW, HEADS, N), F32),
        V_((ROW, T, T), F32),
        V_((ROW, T, T), F32),
        V_((ROW, T, T), F32),
        V_((CHUNKS, ROW + 1, CW, N), F32),
        V_((CHUNKS, ROW + 1, CW, N), F32),
        V_((CHUNKS, ROW, CW, T), F32),
        V_((ROW, T, T), F32),
        V_((ROW, HEADS, T), F32),
        V_((ROW, T, T), F32),
        V_((ROW, HEADS, T), F32),
        V_((ROW, HEADS, T), F32),
        V_((ROW, HEADS, T), F32),
        V_((CHUNKS, CW, N), BF16),
        V_((CHUNKS, CW, N), BF16),
        V_((CHUNKS, CW, N), BF16),
        V_((CHUNKS, CW, N), BF16),
        V_((ROW, T, N), F32),
        V_((ROW, T, N), F32),
        V_((ROW, 2, T, N), BF16),
        V_((2, 2, 2, T, N), BF16),
        V_((CHUNKS, ROW, CW, T), BF16),
        V_((ROW, HEADS, T), F32),
        V_((ROW, HEADS, T), F32),
        pltpu.SemaphoreType.DMA((112,)),
        pltpu.SemaphoreType.DMA((9,)),
        pltpu.SemaphoreType.DMA((CHUNKS,)),
        pltpu.SemaphoreType.DMA((CHUNKS,)),
        pltpu.SemaphoreType.DMA((CHUNKS,)),
        pltpu.SemaphoreType.DMA((CHUNKS,)),
    ]
    gf, gs, gd, gim, gom = pl.pallas_call(
        kernel,
        out_shape=(
            jax.ShapeDtypeStruct((64 * W, T), BF16),
            jax.ShapeDtypeStruct((64, T), F32),
            jax.ShapeDtypeStruct((64, T), F32),
            jax.ShapeDtypeStruct((2, T, N), F32),
            jax.ShapeDtypeStruct((2, T, N), F32),
        ),
        in_specs=[any_, vmem, vmem, vmem, vmem, any_],
        out_specs=(any_, vmem, vmem, vmem, vmem),
        scratch_shapes=scratch,
        compiler_params=pltpu.CompilerParams(
            collective_id=0, has_side_effects=True, vmem_limit_bytes=50 * 2**20
        ),
        name="ssd_backward",
    )(feat, step, dec, maps, seg, grad)
    return (
        jnp.transpose(gf.reshape(64, W, T), (2, 0, 1))[None],
        gs.T[None],
        gd.T[None],
        jnp.transpose(gim, (1, 0, 2))[None],
        jnp.transpose(gom, (1, 0, 2))[None],
    )


def solution(mesh):
    placed = (
        P("section", "seq", "head", None),
        P("section", "seq", "head"),
        P("section", "seq", "head"),
        P("section", "seq", "head", None),
        P("section", "seq", "head", None),
        P("section", "seq"),
        P("section", ("seq", "head"), None),
    )
    return jax.shard_map(
        per_device,
        mesh=mesh,
        in_specs=placed,
        out_specs=(
            P("section", "seq", "head", None),
            P("section", "seq", "head"),
            P("section", "seq", "head"),
            P("section", "seq", "head", None),
            P("section", "seq", "head", None),
        ),
        check_vma=False,
    )
```

```python
import itertools

import jax
import jax.numpy as jnp
from jax import lax
from jax.experimental import pallas as pl
from jax.experimental.pallas import tpu as pltpu
from jax.sharding import PartitionSpec as P

MESH = pl.DeviceIdType.MESH
F32 = jnp.float32
BF16 = jnp.bfloat16
HIGHEST = lax.Precision.HIGHEST

T = 128
W = 64
N = 256
ROW = 4
HEADS = 16
CHUNKS = 8
HC = HEADS // CHUNKS
WINDOW = 3
LAG = 2
CW = HC * W
FBASE = 40 + 8 * CHUNKS


def dot(a, b, precision=None):
    return lax.dot_general(
        a, b, (((1,), (0,)), ((), ())), precision=precision, preferred_element_type=F32
    )


def dot_nt(a, b, precision=None):
    return lax.dot_general(
        a, b, (((1,), (1,)), ((), ())), precision=precision, preferred_element_type=F32
    )


def dot_tn(a, b):
    return lax.dot_general(a, b, (((0,), (0,)), ((), ())), preferred_element_type=F32)


def place(s, y, x, c):
    return {
        "section": lax.rem(s + 8, 8),
        "seq": lax.rem(y + 4, 4) * 4 + lax.rem(x + 4, 4),
        "head": lax.rem(c, 2),
    }


def kernel(
    feat, step, dec, map_in, map_out, seg, grad,
    gf_out, gs_out, gd_out, PM,
    XT, XW, GRN, GRT, GHW, MAP, STEP, DEC, SEG, PREV,
    L, LT, HW, TW, STW, DB, CF, CB, CM, MASK, PRE,
    PF, PB, VI, WS, CK, RK, U, V, B4,
    RF, RB, ES, GS, EA, GA, EB, COF, COB, RDEC, ROWD,
    GIM, GOM, PMS, GF, GSS, GDS, SEGI, SEGF, RAW, MAPS,
    ssem, rs_one, ss_grad, rs_feat, rs_grad, rs_f, rs_b, ready,
):
    s = lax.axis_index("section")
    q = lax.axis_index("seq")
    c = lax.axis_index("head")
    y = q // 4
    x = lax.rem(q, 4)
    first_head = 16 * x
    R_SEG, R_STEP, R_DEC, R_MAP, R_PREV, R_GF, R_GS, R_GD, R_PM, R_RD, R_A, R_B, R_C = range(13)

    barrier = pltpu.get_barrier_semaphore()
    load_seg = pltpu.make_async_copy(seg, SEGI, rs_one.at[R_A])
    load_in = pltpu.make_async_copy(map_in, RAW.at[0], rs_one.at[R_B])
    load_out = pltpu.make_async_copy(map_out, RAW.at[1], rs_one.at[R_C])
    load_seg.start()
    load_in.start()
    load_out.start()

    def greet(target):
        pl.semaphore_signal(barrier, inc=1, device_id=target, device_id_type=MESH)

    for dx in range(1, 4):
        greet(place(s, y, x + dx, 0))

    @pl.when(c == 1)
    def _():
        greet(place(s, y, x, 0))

    for dx in range(4):
        greet(place(s + 1, y, x + dx, 1))
    for dy in range(1, 4):
        greet(place(s, y + dy, x, 1))

    load_seg.wait()
    SEGF[...] = jnp.broadcast_to(SEGI[...].astype(F32), (8, T))
    load_in.wait()
    load_out.wait()
    for g in range(2):
        MAPS[g, 0] = RAW[0, :, g, :]
        MAPS[g, 1] = RAW[1, :, g, :]

    @pl.when(c == 0)
    def _():
        pl.semaphore_wait(barrier, 7)
        pl.semaphore_signal(ready, inc=1, device_id=place(s, y, x, 1), device_id_type=MESH)

    @pl.when(c == 1)
    def _():
        pl.semaphore_wait(ready, 1)

    pending = []
    count = itertools.count()

    def send(src, dst, rsem, target):
        copy = pltpu.make_async_remote_copy(
            src_ref=src, dst_ref=dst, send_sem=ssem.at[next(count)], recv_sem=rsem,
            device_id=target, device_id_type=MESH,
        )
        copy.start()
        pending.append(copy)

    def arrived(ref, sem):
        pltpu.make_async_copy(ref, ref, sem).wait()

    pltpu.make_async_copy(SEGF, SEG.at[x], rs_one.at[R_SEG]).start()
    for dx in range(1, 4):
        send(SEGF, SEG.at[x], rs_one.at[R_SEG], place(s, y, x + dx, c))
    workers = [lax.rem(x + dx, 4) for dx in range(4)]

    def to_worker(src, dst, rsem, dx):
        if dx == 0:
            pltpu.make_async_copy(src, dst, rsem).start()
        else:
            send(src, dst, rsem, place(s, y, workers[dx], c))

    for dx in range(4):
        rows = pl.ds(pl.multiple_of(16 * workers[dx], 16), 16)
        to_worker(step.at[rows], STEP.at[x], rs_one.at[R_STEP], dx)
        to_worker(dec.at[rows], DEC.at[x], rs_one.at[R_DEC], dx)
    for dx in range(4):
        to_worker(MAPS.at[workers[dx] // 2], MAP.at[x], rs_one.at[R_MAP], dx)
    feat_sends = {}

    def issue_feat(k):
        before = len(pending)
        for dx in range(4):
            rows = pl.ds(pl.multiple_of((16 * workers[dx] + HC * k) * W, CW), CW)
            to_worker(feat.at[rows], XT.at[k, x], rs_feat.at[k], dx)
        feat_sends[k] = pending[before:]
        del pending[before:]

    def issue_grad(k):
        for dx in range(4):
            for dc in range(2):
                xw = lax.rem(x + dx, 4)
                cw = lax.rem(c + dc, 2)
                cols = pl.ds(pl.multiple_of((64 * cw + 16 * xw + HC * k) * W, CW), CW)
                pltpu.make_async_remote_copy(
                    src_ref=grad.at[:, cols],
                    dst_ref=GRN.at[k, x, pl.ds(pl.multiple_of(64 * c, 64), 64), :],
                    send_sem=ss_grad.at[k],
                    recv_sem=rs_grad.at[k],
                    device_id=place(s - 1, y, xw, cw),
                    device_id_type=MESH,
                ).start()

    def gone(k):
        for copy in feat_sends[k]:
            copy.wait_send()
        arrived(grad.at[:, pl.ds(0, 8 * CW)], ss_grad.at[k])

    for k in range(WINDOW):
        issue_feat(k)

    @pl.when(c == 1)
    def _():
        pl.semaphore_wait(barrier, 14)
        pl.semaphore_signal(ready, inc=1, device_id=place(s, y, x, 0), device_id_type=MESH)

    @pl.when(c == 0)
    def _():
        pl.semaphore_wait(ready, 1)

    for k in range(WINDOW):
        issue_grad(k)

    arrived(SEG, rs_one.at[R_SEG])
    send(SEG.at[3], PREV, rs_one.at[R_PREV], place(s, y + 1, x, c))
    arrived(STEP, rs_one.at[R_STEP])
    arrived(DEC, rs_one.at[R_DEC])
    row_id = lax.broadcasted_iota(jnp.int32, (T, T), 0)
    col_id = lax.broadcasted_iota(jnp.int32, (T, T), 1)
    upper = (row_id <= col_id).astype(F32)
    for b in range(ROW):
        total = dot(DEC[b], upper, HIGHEST)
        L[b] = total
        padded = jnp.concatenate([total, jnp.zeros((T - HEADS, T), F32)], axis=0)
        LT[b] = jnp.transpose(padded)
        seg_row = SEG[b][0:1, :]
        seg_col = jnp.transpose(jnp.broadcast_to(seg_row, (T, T)))
        same = (seg_col == seg_row).astype(F32)
        MASK[b] = jnp.where(row_id >= col_id, same, 0.0)
        PRE[b] = jnp.where(row_id < col_id, same, 0.0)
    arrived(PREV, rs_one.at[R_PREV])
    first = (y > 0).astype(F32)
    decays = []
    for b in range(ROW):
        total = L[b]
        seg_row = SEG[b][0:1, :]
        if b == 0:
            previous = PREV[0:1, T - 1 : T] * first
        else:
            previous = SEG[b - 1][0:1, T - 1 : T]
        last = total[:, T - 1 : T]
        seg_last = seg_row[:, T - 1 : T]
        carried = (seg_row == previous).astype(F32)
        tail = (seg_row == seg_last).astype(F32)
        HW[b] = carried * jnp.exp(total)
        tw = tail * jnp.exp(last - total)
        TW[b] = tw
        STW[b] = STEP[b] * tw
        d = jnp.broadcast_to((seg_last == previous).astype(F32) * jnp.exp(last), (HEADS, N))
        DB[b] = d
        decays.append(d)
    one = jnp.ones((HEADS, N), F32)
    run = one
    for b in range(ROW):
        CF[b] = run
        run = run * decays[b]
    CF[ROW] = run
    run = one
    for b in reversed(range(ROW)):
        CB[b] = run
        run = run * decays[b]
    ROWD[...] = CF[ROW][:, 0:T]
    pltpu.make_async_copy(ROWD, RDEC.at[y], rs_one.at[R_RD]).start()
    for dy in range(1, 4):
        send(ROWD, RDEC.at[y], rs_one.at[R_RD], place(s, y + dy, x, c))
    arrived(MAP, rs_one.at[R_MAP])
    for b in range(ROW):
        CM[b] = dot_nt(MAP[b, 1], MAP[b, 0])
        WS[b] = jnp.zeros((T, T), F32)
        RK[b] = jnp.zeros((T, T), F32)
        GIM[b] = jnp.zeros((T, N), F32)
        GOM[b] = jnp.zeros((T, N), F32)

    def by_head(a):
        return a.reshape(HC, W, a.shape[-1])

    def scaled(a, w):
        return (by_head(a) * w[:, None, :]).reshape(a.shape)

    def heads_of(ref, b, k):
        return ref[b, HC * k : HC * (k + 1), :]

    def copy_f(k, to):
        return pltpu.make_async_remote_copy(
            src_ref=ES.at[k], dst_ref=RF.at[k, y], send_sem=ssem.at[FBASE + 6 * k + to - 1],
            recv_sem=rs_f.at[k, y], device_id=place(s, to, x, c), device_id_type=MESH,
        )

    def copy_b(k, to):
        return pltpu.make_async_remote_copy(
            src_ref=GS.at[k], dst_ref=RB.at[k, y - 1], send_sem=ssem.at[FBASE + 6 * k + 3 + to],
            recv_sem=rs_b.at[k, y - 1], device_id=place(s, to, x, c), device_id_type=MESH,
        )

    def local_states(k):
        arrived(XT.at[k], rs_feat.at[k])
        total = jnp.zeros((CW, N), F32)
        PF[k, 0] = total
        for b in range(ROW):
            xw = scaled(XT[k, b].astype(F32), heads_of(STW, b, k)).astype(BF16)
            XW[k, b] = xw
            total = scaled(total, heads_of(DB, b, k)) + dot(xw, MAP[b, 0])
            PF[k, b + 1] = total
        ES[k] = total.astype(BF16)
        for to in range(1, 4):
            @pl.when(y < to)
            def _(to=to):
                copy_f(k, to).start()

    def local_grads(k):
        arrived(GRN.at[k], rs_grad.at[k])
        total = jnp.zeros((CW, N), F32)
        PB[k, ROW] = total
        for b in reversed(range(ROW)):
            gt = jnp.transpose(GRN[k, b])
            GRT[k, b] = gt
            gh = scaled(gt.astype(F32), heads_of(HW, b, k)).astype(BF16)
            GHW[k, b] = gh
            total = scaled(total, heads_of(DB, b, k)) + dot(gh, MAP[b, 1])
            PB[k, b] = total
        GS[k] = total.astype(BF16)
        for to in range(3):
            @pl.when(y > to)
            def _(to=to):
                copy_b(k, to).start()

    def enter_f(k):
        EA[...] = jnp.zeros((CW, N), F32)
        for src in range(3):
            @pl.when(y > src)
            def _(src=src):
                arrived(RF.at[k, src], rs_f.at[k, src])
                coef = COF[src, HC * k : HC * (k + 1), :]
                EA[...] += scaled(RF[k, src].astype(F32), coef)

    def enter_b(k):
        GA[...] = jnp.zeros((CW, N), F32)
        for src in range(1, 4):
            @pl.when(y < src)
            def _(src=src):
                arrived(RB.at[k, src - 1], rs_b.at[k, src - 1])
                coef = COB[src - 1, HC * k : HC * (k + 1), :]
                GA[...] += scaled(RB[k, src - 1].astype(F32), coef)

    def intra(k):
        def one_block(b, carry):
            xt = XT[k, b]
            zero = jnp.zeros((W, T), BF16)
            spread = jnp.concatenate(
                [
                    jnp.concatenate(
                        [xt[W * h : W * (h + 1)] if h == j else zero for j in range(HC)], axis=1
                    )
                    for h in range(HC)
                ],
                axis=0,
            )
            pairs = dot(GRN[k, b], spread)
            mask = MASK[b] > 0.0
            cross = CM[b]
            columns = LT[b]
            held = WS[b]
            sums = RK[b]
            lane = lax.broadcasted_iota(jnp.int32, (T, T), 1)
            cols = []
            for h in range(HC):
                head = HC * k + h
                gap = columns[:, head : head + 1] - L[b, head : head + 1, :]
                m = jnp.where(mask, jnp.exp(gap), 0.0)
                a = (m * cross).astype(BF16)
                VI[k, b, W * h : W * (h + 1), :] = dot(GRT[k, b, W * h : W * (h + 1), :], a)
                wh = m * pairs[:, T * h : T * (h + 1)] * STEP[b, head : head + 1, :]
                held = held + wh
                kk = wh * cross
                cols.append(jnp.sum(kk, axis=0, keepdims=True))
                sums = jnp.where(lane == head, jnp.sum(kk, axis=1, keepdims=True), sums)
            CK[b, HC * k : HC * (k + 1), :] = jnp.concatenate(cols, axis=0)
            WS[b] = held
            RK[b] = sums
            return carry

        lax.fori_loop(0, ROW, one_block, 0)

    def row_factors():
        arrived(RDEC, rs_one.at[R_RD])
        one = jnp.ones((HEADS, T), F32)
        for src in range(3):
            coef = one
            for r in range(src + 1, 3):
                coef = coef * jnp.where(y > r, RDEC[r], one)
            COF[src] = jnp.concatenate([coef, coef], axis=1)
            coef = one
            for r in range(1, src + 1):
                coef = coef * jnp.where(y < r, RDEC[r], one)
            COB[src] = jnp.concatenate([coef, coef], axis=1)

    def finish_f(k):
        enter_f(k)

        def one_block(b, carry):
            eb = (PF[k, b] + scaled(EA[...], heads_of(CF, b, k))).astype(BF16)
            EB[k, b] = eb
            seen = dot_nt(eb, MAP[b, 1])
            hs = slice(HC * k, HC * (k + 1))
            U[b, hs, :] = heads_of(HW, b, k) * jnp.sum(by_head(GRT[k, b].astype(F32) * seen), axis=1)
            GOM[b] += dot_tn(GHW[k, b], eb)
            return carry

        lax.fori_loop(0, ROW, one_block, 0)

    def finish_b(k):
        enter_b(k)

        def one_block(b, carry):
            gb = (PB[k, b + 1] + scaled(GA[...], heads_of(CB, b, k))).astype(BF16)
            lift = dot_nt(gb, MAP[b, 0])
            val = VI[k, b] + scaled(lift, heads_of(TW, b, k))
            GF[k, b] = scaled(val, heads_of(STEP, b, k)).astype(BF16)
            hs = slice(HC * k, HC * (k + 1))
            V[b, hs, :] = heads_of(STW, b, k) * jnp.sum(by_head(XT[k, b].astype(F32) * lift), axis=1)
            both = jnp.sum(by_head(EB[k, b].astype(F32) * gb.astype(F32)), axis=1)
            B4[b, hs, :] = jnp.broadcast_to(jnp.sum(both, axis=1, keepdims=True), (HC, T))
            GIM[b] += dot_tn(XW[k, b], gb)
            return carry

        lax.fori_loop(0, ROW, one_block, 0)
        for dx in range(4):
            rows = pl.ds(pl.multiple_of((first_head + HC * k) * W, CW), CW)
            to_worker(GF.at[k, workers[dx]], gf_out.at[rows], rs_one.at[R_GF], dx)

    def send_map(m):
        for dx in range(4):
            to_worker(PMS.at[workers[dx], m], PM.at[x // 2, lax.rem(x, 2), m], rs_one.at[R_PM], dx)

    for k in range(CHUNKS):
        local_states(k)
        local_grads(k)
        gone(k)
        if k + WINDOW < CHUNKS:
            issue_feat(k + WINDOW)
            issue_grad(k + WINDOW)
        intra(k)
        if k == 0:
            row_factors()
        if k >= LAG:
            finish_f(k - LAG)
            finish_b(k - LAG)
    for k in range(CHUNKS - LAG, CHUNKS):
        finish_f(k)
        if k + 1 == CHUNKS:
            for b in range(ROW):
                PMS[b, 1] = (GOM[b] + dot(WS[b].astype(BF16), MAP[b, 0])).astype(BF16)
            send_map(1)
        finish_b(k)
    for b in range(ROW):
        PMS[b, 0] = (GIM[b] + dot_tn(WS[b].astype(BF16), MAP[b, 1])).astype(BF16)
    send_map(0)

    for b in range(ROW):
        row_sums = jnp.transpose(RK[b])[0:HEADS, :]
        ck = CK[b]
        v = V[b]
        GSS[b] = (ck + v) / STEP[b]
        chain = dot(row_sums - ck + U[b], MASK[b], HIGHEST) + dot(v, PRE[b], HIGHEST)
        GDS[b] = chain + HW[b] * TW[b] * B4[b]
    for dx in range(4):
        rows = pl.ds(pl.multiple_of(first_head, 16), 16)
        to_worker(GSS.at[workers[dx]], gs_out.at[rows], rs_one.at[R_GS], dx)
        to_worker(GDS.at[workers[dx]], gd_out.at[rows], rs_one.at[R_GD], dx)

    arrived(PM, rs_one.at[R_PM])
    arrived(gf_out, rs_one.at[R_GF])
    arrived(gs_out, rs_one.at[R_GS])
    arrived(gd_out, rs_one.at[R_GD])
    assert next(count) <= FBASE
    for copy in pending:
        copy.wait_send()
    for k in range(CHUNKS):
        for to in range(1, 4):
            @pl.when(y < to)
            def _():
                copy_f(k, to).wait_send()
        for to in range(3):
            @pl.when(y > to)
            def _():
                copy_b(k, to).wait_send()


def settle(gf, gs, gd, pm, gf_out, gs_out, gd_out, gim_out, gom_out, sem):
    copies = [
        pltpu.make_async_copy(a, b, sem.at[i])
        for i, (a, b) in enumerate(((gf, gf_out), (gs, gs_out), (gd, gd_out)))
    ]
    for copy in copies:
        copy.start()
    for g in range(2):
        gim_out[:, g, :] = pm[g, 0, 0].astype(F32) + pm[g, 1, 0].astype(F32)
        gom_out[:, g, :] = pm[g, 0, 1].astype(F32) + pm[g, 1, 1].astype(F32)
    for copy in copies:
        copy.wait()


def per_device(features, step_size, log_decay, input_map, output_map, segment, sent_grad):
    feat = jnp.transpose(features[0], (1, 2, 0)).reshape(64 * W, T)
    step = step_size[0].T
    dec = log_decay[0].T
    grad = sent_grad[0]
    any_ = pl.BlockSpec(memory_space=pltpu.HBM)
    vmem = pl.BlockSpec(memory_space=pltpu.VMEM)
    V_ = pltpu.VMEM
    scratch = [
        V_((CHUNKS, ROW, CW, T), BF16),
        V_((CHUNKS, ROW, CW, T), BF16),
        V_((CHUNKS, ROW, T, CW), BF16),
        V_((CHUNKS, ROW, CW, T), BF16),
        V_((CHUNKS, ROW, CW, T), BF16),
        V_((ROW, 2, T, N), BF16),
        V_((ROW, HEADS, T), F32),
        V_((ROW, HEADS, T), F32),
        V_((ROW, 8, T), F32),
        V_((8, T), F32),
        V_((ROW, HEADS, T), F32),
        V_((ROW, T, T), F32),
        V_((ROW, HEADS, T), F32),
        V_((ROW, HEADS, T), F32),
        V_((ROW, HEADS, T), F32),
        V_((ROW, HEADS, N), F32),
        V_((ROW + 1, HEADS, N), F32),
        V_((ROW, HEADS, N), F32),
        V_((ROW, T, T), F32),
        V_((ROW, T, T), F32),
        V_((ROW, T, T), F32),
        V_((CHUNKS, ROW + 1, CW, N), F32),
        V_((CHUNKS, ROW + 1, CW, N), F32),
        V_((CHUNKS, ROW, CW, T), F32),
        V_((ROW, T, T), F32),
        V_((ROW, HEADS, T), F32),
        V_((ROW, T, T), F32),
        V_((ROW, HEADS, T), F32),
        V_((ROW, HEADS, T), F32),
        V_((ROW, HEADS, T), F32),
        V_((CHUNKS, 3, CW, N), BF16),
        V_((CHUNKS, 3, CW, N), BF16),
        V_((CHUNKS, CW, N), BF16),
        V_((CHUNKS, CW, N), BF16),
        V_((CW, N), F32),
        V_((CW, N), F32),
        V_((CHUNKS, ROW, CW, N), BF16),
        V_((3, HEADS, N), F32),
        V_((3, HEADS, N), F32),
        V_((4, HEADS, T), F32),
        V_((HEADS, T), F32),
        V_((ROW, T, N), F32),
        V_((ROW, T, N), F32),
        V_((ROW, 2, T, N), BF16),
        V_((CHUNKS, ROW, CW, T), BF16),
        V_((ROW, HEADS, T), F32),
        V_((ROW, HEADS, T), F32),
        V_((1, T), jnp.int32),
        V_((8, T), F32),
        V_((2, T, 2, N), BF16),
        V_((2, 2, T, N), BF16),
        pltpu.SemaphoreType.DMA((FBASE + 6 * CHUNKS,)),
        pltpu.SemaphoreType.DMA((13,)),
        pltpu.SemaphoreType.DMA((CHUNKS,)),
        pltpu.SemaphoreType.DMA((CHUNKS,)),
        pltpu.SemaphoreType.DMA((CHUNKS,)),
        pltpu.SemaphoreType.DMA((CHUNKS, 3)),
        pltpu.SemaphoreType.DMA((CHUNKS, 3)),
        pltpu.SemaphoreType.REGULAR,
    ]
    gf, gs, gd, pm = pl.pallas_call(
        kernel,
        out_shape=(
            jax.ShapeDtypeStruct((64 * W, T), BF16),
            jax.ShapeDtypeStruct((64, T), F32),
            jax.ShapeDtypeStruct((64, T), F32),
            jax.ShapeDtypeStruct((2, 2, 2, T, N), BF16),
        ),
        in_specs=[any_] * 7,
        out_specs=(any_, any_, any_, any_),
        scratch_shapes=scratch,
        compiler_params=pltpu.CompilerParams(
            collective_id=0, has_side_effects=True, vmem_limit_bytes=60 * 2**20
        ),
        name="ssd_backward",
    )(feat, step, dec, input_map[0], output_map[0], segment, grad)
    gf, gs, gd, gim, gom = pl.pallas_call(
        settle,
        out_shape=(
            jax.ShapeDtypeStruct((64 * W, T), BF16),
            jax.ShapeDtypeStruct((64, T), F32),
            jax.ShapeDtypeStruct((64, T), F32),
            jax.ShapeDtypeStruct((T, 2, N), F32),
            jax.ShapeDtypeStruct((T, 2, N), F32),
        ),
        in_specs=[any_, any_, any_, vmem],
        out_specs=(vmem,) * 5,
        scratch_shapes=[pltpu.SemaphoreType.DMA((3,))],
        name="settle",
    )(gf, gs, gd, pm)
    return (
        jnp.transpose(gf.reshape(64, W, T), (2, 0, 1))[None],
        gs.T[None],
        gd.T[None],
        gim[None],
        gom[None],
    )


def solution(mesh):
    placed = (
        P("section", "seq", "head", None),
        P("section", "seq", "head"),
        P("section", "seq", "head"),
        P("section", "seq", "head", None),
        P("section", "seq", "head", None),
        P("section", "seq"),
        P("section", ("seq", "head"), None),
    )
    return jax.shard_map(
        per_device,
        mesh=mesh,
        in_specs=placed,
        out_specs=(
            P("section", "seq", "head", None),
            P("section", "seq", "head"),
            P("section", "seq", "head"),
            P("section", "seq", "head", None),
            P("section", "seq", "head", None),
        ),
        check_vma=False,
    )
```

```python
import itertools

import jax
import jax.numpy as jnp
from jax import lax
from jax.experimental import pallas as pl
from jax.experimental.pallas import tpu as pltpu
from jax.sharding import PartitionSpec as P

MESH = pl.DeviceIdType.MESH
F32 = jnp.float32
BF16 = jnp.bfloat16
HIGHEST = lax.Precision.HIGHEST

T = 128
W = 64
N = 256
ROW = 4
HEADS = 16
CHUNKS = 8
HC = HEADS // CHUNKS
WINDOW = 3
PIECES = 4
LAG = 2
CW = HC * W
FBASE = 40 + 8 * CHUNKS


def dot(a, b, precision=None):
    return lax.dot_general(
        a, b, (((1,), (0,)), ((), ())), precision=precision, preferred_element_type=F32
    )


def dot_nt(a, b, precision=None):
    return lax.dot_general(
        a, b, (((1,), (1,)), ((), ())), precision=precision, preferred_element_type=F32
    )


def dot_tn(a, b):
    return lax.dot_general(a, b, (((0,), (0,)), ((), ())), preferred_element_type=F32)


def place(s, y, x, c):
    return {
        "section": lax.rem(s + 8, 8),
        "seq": lax.rem(y + 4, 4) * 4 + lax.rem(x + 4, 4),
        "head": lax.rem(c, 2),
    }


def kernel(
    feat, step, dec, map_in, map_out, seg, grad,
    gf_out, gs_out, gd_out, PM,
    XT, XW, GRN, GRT, GHW, MAP, STEP, DEC, SEG, PREV,
    L, LT, HW, TW, STW, DB, CF, CB, CM, MASK, PRE,
    PF, PB, VI, WS, CK, RK, U, V, B4,
    RF, RB, ES, GS, EA, GA, EB, COF, COB, RDEC, ROWD,
    GIM, GOM, PMS, GF, GSS, GDS, SEGI, SEGF, RAW, MAPS, MAPT,
    ssem, rs_one, ss_grad, rs_feat, rs_grad, rs_f, rs_b, ready,
):
    s = lax.axis_index("section")
    q = lax.axis_index("seq")
    c = lax.axis_index("head")
    y = q // 4
    x = lax.rem(q, 4)
    first_head = 16 * x
    R_SEG, R_STEP, R_DEC, R_MAP, R_PREV, R_GF, R_GS, R_GD, R_PM, R_RD, R_A, R_B, R_C = range(13)

    barrier = pltpu.get_barrier_semaphore()
    load_seg = pltpu.make_async_copy(seg, SEGI, rs_one.at[R_A])
    load_in = pltpu.make_async_copy(map_in, RAW.at[0], rs_one.at[R_B])
    load_out = pltpu.make_async_copy(map_out, RAW.at[1], rs_one.at[R_C])
    load_seg.start()
    load_in.start()
    load_out.start()

    def greet(target):
        pl.semaphore_signal(barrier, inc=1, device_id=target, device_id_type=MESH)

    for dx in range(1, 4):
        greet(place(s, y, x + dx, 0))

    @pl.when(c == 1)
    def _():
        greet(place(s, y, x, 0))

    for dx in range(4):
        greet(place(s + 1, y, x + dx, 1))
    for dy in range(1, 4):
        greet(place(s, y + dy, x, 1))

    load_seg.wait()
    SEGF[...] = jnp.broadcast_to(SEGI[...].astype(F32), (8, T))
    load_in.wait()
    load_out.wait()
    for g in range(2):
        MAPS[g, 0] = RAW[0, :, g, :]
        MAPS[g, 1] = RAW[1, :, g, :]

    @pl.when(c == 0)
    def _():
        pl.semaphore_wait(barrier, 7)
        pl.semaphore_signal(ready, inc=1, device_id=place(s, y, x, 1), device_id_type=MESH)

    @pl.when(c == 1)
    def _():
        pl.semaphore_wait(ready, 1)

    pending = []
    count = itertools.count()

    def send(src, dst, rsem, target):
        copy = pltpu.make_async_remote_copy(
            src_ref=src, dst_ref=dst, send_sem=ssem.at[next(count)], recv_sem=rsem,
            device_id=target, device_id_type=MESH,
        )
        copy.start()
        pending.append(copy)

    def arrived(ref, sem):
        pltpu.make_async_copy(ref, ref, sem).wait()

    pltpu.make_async_copy(SEGF, SEG.at[x], rs_one.at[R_SEG]).start()
    for dx in range(1, 4):
        send(SEGF, SEG.at[x], rs_one.at[R_SEG], place(s, y, x + dx, c))
    workers = [lax.rem(x + dx, 4) for dx in range(4)]

    def to_worker(src, dst, rsem, dx):
        if dx == 0:
            pltpu.make_async_copy(src, dst, rsem).start()
        else:
            send(src, dst, rsem, place(s, y, workers[dx], c))

    for dx in range(4):
        rows = pl.ds(pl.multiple_of(16 * workers[dx], 16), 16)
        to_worker(step.at[rows], STEP.at[x], rs_one.at[R_STEP], dx)
        to_worker(dec.at[rows], DEC.at[x], rs_one.at[R_DEC], dx)
    for dx in range(4):
        to_worker(MAPS.at[workers[dx] // 2], MAP.at[x], rs_one.at[R_MAP], dx)
    feat_sends = {}

    def issue_feat(k):
        before = len(pending)
        for dx in range(4):
            rows = pl.ds(pl.multiple_of((16 * workers[dx] + HC * k) * W, CW), CW)
            to_worker(feat.at[rows], XT.at[k, x], rs_feat.at[k], dx)
        feat_sends[k] = pending[before:]
        del pending[before:]

    def issue_grad(k):
        for dx in range(4):
            for dc in range(2):
                xw = lax.rem(x + dx, 4)
                cw = lax.rem(c + dc, 2)
                cols = pl.ds(pl.multiple_of((64 * cw + 16 * xw + HC * k) * W, CW), CW)
                pltpu.make_async_remote_copy(
                    src_ref=grad.at[:, cols],
                    dst_ref=GRN.at[k, x, pl.ds(pl.multiple_of(64 * c, 64), 64), :],
                    send_sem=ss_grad.at[k],
                    recv_sem=rs_grad.at[k],
                    device_id=place(s - 1, y, xw, cw),
                    device_id_type=MESH,
                ).start()

    def gone(k):
        for copy in feat_sends[k]:
            copy.wait_send()
        arrived(grad.at[:, pl.ds(0, 8 * CW)], ss_grad.at[k])

    for k in range(WINDOW):
        issue_feat(k)

    @pl.when(c == 1)
    def _():
        pl.semaphore_wait(barrier, 14)
        pl.semaphore_signal(ready, inc=1, device_id=place(s, y, x, 0), device_id_type=MESH)

    @pl.when(c == 0)
    def _():
        pl.semaphore_wait(ready, 1)

    for k in range(WINDOW):
        issue_grad(k)

    arrived(SEG, rs_one.at[R_SEG])
    send(SEG.at[3], PREV, rs_one.at[R_PREV], place(s, y + 1, x, c))
    arrived(STEP, rs_one.at[R_STEP])
    arrived(DEC, rs_one.at[R_DEC])
    row_id = lax.broadcasted_iota(jnp.int32, (T, T), 0)
    col_id = lax.broadcasted_iota(jnp.int32, (T, T), 1)
    upper = (row_id <= col_id).astype(F32)
    for b in range(ROW):
        total = dot(DEC[b], upper, HIGHEST)
        L[b] = total
        padded = jnp.concatenate([total, jnp.zeros((T - HEADS, T), F32)], axis=0)
        LT[b] = jnp.transpose(padded)
        seg_row = SEG[b][0:1, :]
        seg_col = jnp.transpose(jnp.broadcast_to(seg_row, (T, T)))
        same = (seg_col == seg_row).astype(F32)
        MASK[b] = jnp.where(row_id >= col_id, same, 0.0)
        PRE[b] = jnp.where(row_id < col_id, same, 0.0)
    arrived(PREV, rs_one.at[R_PREV])
    first = (y > 0).astype(F32)
    decays = []
    for b in range(ROW):
        total = L[b]
        seg_row = SEG[b][0:1, :]
        if b == 0:
            previous = PREV[0:1, T - 1 : T] * first
        else:
            previous = SEG[b - 1][0:1, T - 1 : T]
        last = total[:, T - 1 : T]
        seg_last = seg_row[:, T - 1 : T]
        carried = (seg_row == previous).astype(F32)
        tail = (seg_row == seg_last).astype(F32)
        HW[b] = carried * jnp.exp(total)
        tw = tail * jnp.exp(last - total)
        TW[b] = tw
        STW[b] = STEP[b] * tw
        d = jnp.broadcast_to((seg_last == previous).astype(F32) * jnp.exp(last), (HEADS, N))
        DB[b] = d
        decays.append(d)
    one = jnp.ones((HEADS, N), F32)
    run = one
    for b in range(ROW):
        CF[b] = run
        run = run * decays[b]
    CF[ROW] = run
    run = one
    for b in reversed(range(ROW)):
        CB[b] = run
        run = run * decays[b]
    ROWD[...] = CF[ROW][:, 0:T]
    pltpu.make_async_copy(ROWD, RDEC.at[y], rs_one.at[R_RD]).start()
    for dy in range(1, 4):
        send(ROWD, RDEC.at[y], rs_one.at[R_RD], place(s, y + dy, x, c))
    arrived(MAP, rs_one.at[R_MAP])
    for b in range(ROW):
        MAPT[b, 0] = jnp.transpose(MAP[b, 0])
        MAPT[b, 1] = jnp.transpose(MAP[b, 1])
        CM[b] = dot(MAP[b, 1], MAPT[b, 0])
        WS[b] = jnp.zeros((T, T), F32)
        RK[b] = jnp.zeros((T, T), F32)
        GIM[b] = jnp.zeros((T, N), F32)
        GOM[b] = jnp.zeros((T, N), F32)

    def by_head(a):
        return a.reshape(HC, W, a.shape[-1])

    def scaled(a, w):
        return (by_head(a) * w[:, None, :]).reshape(a.shape)

    def heads_of(ref, b, k):
        return ref[b, HC * k : HC * (k + 1), :]

    def copy_f(k, to):
        return pltpu.make_async_remote_copy(
            src_ref=ES.at[k], dst_ref=RF.at[k, y], send_sem=ssem.at[FBASE + 6 * k + to - 1],
            recv_sem=rs_f.at[k, y], device_id=place(s, to, x, c), device_id_type=MESH,
        )

    def copy_b(k, to):
        return pltpu.make_async_remote_copy(
            src_ref=GS.at[k], dst_ref=RB.at[k, y - 1], send_sem=ssem.at[FBASE + 6 * k + 3 + to],
            recv_sem=rs_b.at[k, y - 1], device_id=place(s, to, x, c), device_id_type=MESH,
        )

    def local_states(k):
        arrived(XT.at[k], rs_feat.at[k])
        total = jnp.zeros((CW, N), F32)
        PF[k, 0] = total
        for b in range(ROW):
            xw = scaled(XT[k, b].astype(F32), heads_of(STW, b, k)).astype(BF16)
            XW[k, b] = xw
            total = scaled(total, heads_of(DB, b, k)) + dot(xw, MAP[b, 0])
            PF[k, b + 1] = total
        ES[k] = total.astype(BF16)
        for to in range(1, 4):
            @pl.when(y < to)
            def _(to=to):
                copy_f(k, to).start()

    def local_grads(k):
        arrived(GRN.at[k], rs_grad.at[k])
        total = jnp.zeros((CW, N), F32)
        PB[k, ROW] = total
        for b in reversed(range(ROW)):
            gt = jnp.transpose(GRN[k, b])
            GRT[k, b] = gt
            gh = scaled(gt.astype(F32), heads_of(HW, b, k)).astype(BF16)
            GHW[k, b] = gh
            total = scaled(total, heads_of(DB, b, k)) + dot(gh, MAP[b, 1])
            PB[k, b] = total
        GS[k] = total.astype(BF16)
        for to in range(3):
            @pl.when(y > to)
            def _(to=to):
                copy_b(k, to).start()

    def enter_f(k):
        EA[...] = jnp.zeros((CW, N), F32)
        for src in range(3):
            @pl.when(y > src)
            def _(src=src):
                arrived(RF.at[k, src], rs_f.at[k, src])
                coef = COF[src, HC * k : HC * (k + 1), :]
                EA[...] += scaled(RF[k, src].astype(F32), coef)

    def enter_b(k):
        GA[...] = jnp.zeros((CW, N), F32)
        for src in range(1, 4):
            @pl.when(y < src)
            def _(src=src):
                arrived(RB.at[k, src - 1], rs_b.at[k, src - 1])
                coef = COB[src - 1, HC * k : HC * (k + 1), :]
                GA[...] += scaled(RB[k, src - 1].astype(F32), coef)

    def intra(k):
        def one_block(b, carry):
            xt = XT[k, b]
            zero = jnp.zeros((W, T), BF16)
            spread = jnp.concatenate(
                [
                    jnp.concatenate(
                        [xt[W * h : W * (h + 1)] if h == j else zero for j in range(HC)], axis=1
                    )
                    for h in range(HC)
                ],
                axis=0,
            )
            pairs = dot(GRN[k, b], spread)
            mask = MASK[b] > 0.0
            cross = CM[b]
            columns = LT[b]
            held = WS[b]
            sums = RK[b]
            lane = lax.broadcasted_iota(jnp.int32, (T, T), 1)
            cols = []
            for h in range(HC):
                head = HC * k + h
                gap = columns[:, head : head + 1] - L[b, head : head + 1, :]
                m = jnp.where(mask, jnp.exp(gap), 0.0)
                a = (m * cross).astype(BF16)
                VI[k, b, W * h : W * (h + 1), :] = dot(GRT[k, b, W * h : W * (h + 1), :], a)
                wh = m * pairs[:, T * h : T * (h + 1)] * STEP[b, head : head + 1, :]
                held = held + wh
                kk = wh * cross
                cols.append(jnp.sum(kk, axis=0, keepdims=True))
                sums = jnp.where(lane == head, jnp.sum(kk, axis=1, keepdims=True), sums)
            CK[b, HC * k : HC * (k + 1), :] = jnp.concatenate(cols, axis=0)
            WS[b] = held
            RK[b] = sums
            return carry

        lax.fori_loop(0, ROW, one_block, 0, unroll=4)

    def row_factors():
        arrived(RDEC, rs_one.at[R_RD])
        one = jnp.ones((HEADS, T), F32)
        for src in range(3):
            coef = one
            for r in range(src + 1, 3):
                coef = coef * jnp.where(y > r, RDEC[r], one)
            COF[src] = jnp.concatenate([coef, coef], axis=1)
            coef = one
            for r in range(1, src + 1):
                coef = coef * jnp.where(y < r, RDEC[r], one)
            COB[src] = jnp.concatenate([coef, coef], axis=1)

    def finish_f(k):
        enter_f(k)

        def one_block(b, carry):
            eb = (PF[k, b] + scaled(EA[...], heads_of(CF, b, k))).astype(BF16)
            EB[k, b] = eb
            seen = dot(eb, MAPT[b, 1])
            hs = slice(HC * k, HC * (k + 1))
            U[b, hs, :] = heads_of(HW, b, k) * jnp.sum(by_head(GRT[k, b].astype(F32) * seen), axis=1)
            GOM[b] += dot_tn(GHW[k, b], eb)
            return carry

        lax.fori_loop(0, ROW, one_block, 0, unroll=4)

    def finish_b(k):
        enter_b(k)

        def one_block(b, carry):
            gb = (PB[k, b + 1] + scaled(GA[...], heads_of(CB, b, k))).astype(BF16)
            lift = dot(gb, MAPT[b, 0])
            val = VI[k, b] + scaled(lift, heads_of(TW, b, k))
            GF[k, b] = scaled(val, heads_of(STEP, b, k)).astype(BF16)
            hs = slice(HC * k, HC * (k + 1))
            V[b, hs, :] = heads_of(STW, b, k) * jnp.sum(by_head(XT[k, b].astype(F32) * lift), axis=1)
            both = jnp.sum(by_head(EB[k, b].astype(F32) * gb.astype(F32)), axis=1)
            B4[b, hs, :] = jnp.broadcast_to(jnp.sum(both, axis=1, keepdims=True), (HC, T))
            GIM[b] += dot_tn(XW[k, b], gb)
            return carry

        lax.fori_loop(0, ROW, one_block, 0, unroll=4)
        for dx in range(4):
            rows = pl.ds(pl.multiple_of((first_head + HC * k) * W, CW), CW)
            to_worker(GF.at[k, workers[dx]], gf_out.at[rows], rs_one.at[R_GF], dx)

    def send_map(m):
        for dx in range(4):
            to_worker(PMS.at[workers[dx], m], PM.at[x // 2, lax.rem(x, 2), m], rs_one.at[R_PM], dx)

    for k in range(CHUNKS):
        local_states(k)
        local_grads(k)
        gone(k)
        if k + WINDOW < CHUNKS:
            issue_feat(k + WINDOW)
            issue_grad(k + WINDOW)
        intra(k)
        if k == 0:
            row_factors()
        if k >= LAG:
            finish_f(k - LAG)
            finish_b(k - LAG)
    for k in range(CHUNKS - LAG, CHUNKS):
        finish_f(k)
        if k + 1 == CHUNKS:
            for b in range(ROW):
                PMS[b, 1] = (GOM[b] + dot(WS[b].astype(BF16), MAP[b, 0])).astype(BF16)
            send_map(1)
        finish_b(k)
    for b in range(ROW):
        PMS[b, 0] = (GIM[b] + dot_tn(WS[b].astype(BF16), MAP[b, 1])).astype(BF16)
    send_map(0)

    for b in range(ROW):
        row_sums = jnp.transpose(RK[b])[0:HEADS, :]
        ck = CK[b]
        v = V[b]
        GSS[b] = (ck + v) / STEP[b]
        chain = dot(row_sums - ck + U[b], MASK[b], HIGHEST) + dot(v, PRE[b], HIGHEST)
        GDS[b] = chain + HW[b] * TW[b] * B4[b]
    for dx in range(4):
        rows = pl.ds(pl.multiple_of(first_head, 16), 16)
        to_worker(GSS.at[workers[dx]], gs_out.at[rows], rs_one.at[R_GS], dx)
        to_worker(GDS.at[workers[dx]], gd_out.at[rows], rs_one.at[R_GD], dx)

    arrived(PM, rs_one.at[R_PM])
    arrived(gf_out, rs_one.at[R_GF])
    arrived(gs_out, rs_one.at[R_GS])
    arrived(gd_out, rs_one.at[R_GD])
    assert next(count) <= FBASE
    for copy in pending:
        copy.wait_send()
    for k in range(CHUNKS):
        for to in range(1, 4):
            @pl.when(y < to)
            def _():
                copy_f(k, to).wait_send()
        for to in range(3):
            @pl.when(y > to)
            def _():
                copy_b(k, to).wait_send()


def settle(
    gf, gs, gd, pm, gf_out, gs_out, gd_out, gim_out, gom_out,
    held, steps, maps, sums, sem_in, sem_out,
):
    size = 64 * W // PIECES
    reads, writes = [], []
    for g in range(2):
        reads.append(pltpu.make_async_copy(pm.at[g], maps.at[g], sem_in.at[g]))
    for i in range(PIECES):
        rows = pl.ds(i * size, size)
        reads.append(pltpu.make_async_copy(gf.at[rows], held.at[rows], sem_in.at[2 + i]))
        writes.append(pltpu.make_async_copy(held.at[rows], gf_out.at[rows], sem_out.at[i]))
    for i, (a, b) in enumerate(((gs, gs_out), (gd, gd_out))):
        reads.append(pltpu.make_async_copy(a, steps.at[i], sem_in.at[2 + PIECES + i]))
        writes.append(pltpu.make_async_copy(steps.at[i], b, sem_out.at[PIECES + i]))
    for copy in reads:
        copy.start()
    for g in range(2):
        reads[g].wait()
        for m in range(2):
            sums[m, :, g, :] = maps[g, 0, m].astype(F32) + maps[g, 1, m].astype(F32)
    for m, out in enumerate((gim_out, gom_out)):
        copy = pltpu.make_async_copy(sums.at[m], out, sem_out.at[PIECES + 2 + m])
        copy.start()
        writes.append(copy)
    for i in range(PIECES + 2):
        reads[2 + i].wait()
        writes[i].start()
    for copy in writes:
        copy.wait()


def per_device(features, step_size, log_decay, input_map, output_map, segment, sent_grad):
    feat = jnp.transpose(features[0], (1, 2, 0)).reshape(64 * W, T)
    step = step_size[0].T
    dec = log_decay[0].T
    grad = sent_grad[0]
    any_ = pl.BlockSpec(memory_space=pltpu.HBM)
    V_ = pltpu.VMEM
    scratch = [
        V_((CHUNKS, ROW, CW, T), BF16),
        V_((CHUNKS, ROW, CW, T), BF16),
        V_((CHUNKS, ROW, T, CW), BF16),
        V_((CHUNKS, ROW, CW, T), BF16),
        V_((CHUNKS, ROW, CW, T), BF16),
        V_((ROW, 2, T, N), BF16),
        V_((ROW, HEADS, T), F32),
        V_((ROW, HEADS, T), F32),
        V_((ROW, 8, T), F32),
        V_((8, T), F32),
        V_((ROW, HEADS, T), F32),
        V_((ROW, T, T), F32),
        V_((ROW, HEADS, T), F32),
        V_((ROW, HEADS, T), F32),
        V_((ROW, HEADS, T), F32),
        V_((ROW, HEADS, N), F32),
        V_((ROW + 1, HEADS, N), F32),
        V_((ROW, HEADS, N), F32),
        V_((ROW, T, T), F32),
        V_((ROW, T, T), F32),
        V_((ROW, T, T), F32),
        V_((CHUNKS, ROW + 1, CW, N), F32),
        V_((CHUNKS, ROW + 1, CW, N), F32),
        V_((CHUNKS, ROW, CW, T), F32),
        V_((ROW, T, T), F32),
        V_((ROW, HEADS, T), F32),
        V_((ROW, T, T), F32),
        V_((ROW, HEADS, T), F32),
        V_((ROW, HEADS, T), F32),
        V_((ROW, HEADS, T), F32),
        V_((CHUNKS, 3, CW, N), BF16),
        V_((CHUNKS, 3, CW, N), BF16),
        V_((CHUNKS, CW, N), BF16),
        V_((CHUNKS, CW, N), BF16),
        V_((CW, N), F32),
        V_((CW, N), F32),
        V_((CHUNKS, ROW, CW, N), BF16),
        V_((3, HEADS, N), F32),
        V_((3, HEADS, N), F32),
        V_((4, HEADS, T), F32),
        V_((HEADS, T), F32),
        V_((ROW, T, N), F32),
        V_((ROW, T, N), F32),
        V_((ROW, 2, T, N), BF16),
        V_((CHUNKS, ROW, CW, T), BF16),
        V_((ROW, HEADS, T), F32),
        V_((ROW, HEADS, T), F32),
        V_((1, T), jnp.int32),
        V_((8, T), F32),
        V_((2, T, 2, N), BF16),
        V_((2, 2, T, N), BF16),
        V_((ROW, 2, N, T), BF16),
        pltpu.SemaphoreType.DMA((FBASE + 6 * CHUNKS,)),
        pltpu.SemaphoreType.DMA((13,)),
        pltpu.SemaphoreType.DMA((CHUNKS,)),
        pltpu.SemaphoreType.DMA((CHUNKS,)),
        pltpu.SemaphoreType.DMA((CHUNKS,)),
        pltpu.SemaphoreType.DMA((CHUNKS, 3)),
        pltpu.SemaphoreType.DMA((CHUNKS, 3)),
        pltpu.SemaphoreType.REGULAR,
    ]
    gf, gs, gd, pm = pl.pallas_call(
        kernel,
        out_shape=(
            jax.ShapeDtypeStruct((64 * W, T), BF16),
            jax.ShapeDtypeStruct((64, T), F32),
            jax.ShapeDtypeStruct((64, T), F32),
            jax.ShapeDtypeStruct((2, 2, 2, T, N), BF16),
        ),
        in_specs=[any_] * 7,
        out_specs=(any_, any_, any_, any_),
        scratch_shapes=scratch,
        compiler_params=pltpu.CompilerParams(
            collective_id=0, has_side_effects=True, vmem_limit_bytes=60 * 2**20
        ),
        name="ssd_backward",
    )(feat, step, dec, input_map[0], output_map[0], segment, grad)
    gf, gs, gd, gim, gom = pl.pallas_call(
        settle,
        out_shape=(
            jax.ShapeDtypeStruct((64 * W, T), BF16),
            jax.ShapeDtypeStruct((64, T), F32),
            jax.ShapeDtypeStruct((64, T), F32),
            jax.ShapeDtypeStruct((T, 2, N), F32),
            jax.ShapeDtypeStruct((T, 2, N), F32),
        ),
        in_specs=[any_] * 4,
        out_specs=(any_,) * 5,
        scratch_shapes=[
            V_((64 * W, T), BF16),
            V_((2, 64, T), F32),
            V_((2, 2, 2, T, N), BF16),
            V_((2, T, 2, N), F32),
            pltpu.SemaphoreType.DMA((PIECES + 4,)),
            pltpu.SemaphoreType.DMA((PIECES + 4,)),
        ],
        compiler_params=pltpu.CompilerParams(vmem_limit_bytes=60 * 2**20),
        name="settle",
    )(gf, gs, gd, pm)
    return (
        jnp.transpose(gf.reshape(64, W, T), (2, 0, 1))[None],
        gs.T[None],
        gd.T[None],
        gim[None],
        gom[None],
    )


def solution(mesh):
    placed = (
        P("section", "seq", "head", None),
        P("section", "seq", "head"),
        P("section", "seq", "head"),
        P("section", "seq", "head", None),
        P("section", "seq", "head", None),
        P("section", "seq"),
        P("section", ("seq", "head"), None),
    )
    return jax.shard_map(
        per_device,
        mesh=mesh,
        in_specs=placed,
        out_specs=(
            P("section", "seq", "head", None),
            P("section", "seq", "head"),
            P("section", "seq", "head"),
            P("section", "seq", "head", None),
            P("section", "seq", "head", None),
        ),
        check_vma=False,
    )
```

```python
import itertools

import jax
import jax.numpy as jnp
from jax import lax
from jax.experimental import pallas as pl
from jax.experimental.pallas import tpu as pltpu
from jax.sharding import PartitionSpec as P

MESH = pl.DeviceIdType.MESH
F32 = jnp.float32
BF16 = jnp.bfloat16
HIGHEST = lax.Precision.HIGHEST

T = 128
W = 64
N = 256
ROW = 4
HEADS = 16
CHUNKS = 8
HC = HEADS // CHUNKS
WINDOW = 3
PIECES = 4
LAG = 2
CW = HC * W
FBASE = 48 + 8 * CHUNKS


def dot(a, b, precision=None):
    return lax.dot_general(
        a, b, (((1,), (0,)), ((), ())), precision=precision, preferred_element_type=F32
    )


def dot_nt(a, b, precision=None):
    return lax.dot_general(
        a, b, (((1,), (1,)), ((), ())), precision=precision, preferred_element_type=F32
    )


def dot_tn(a, b):
    return lax.dot_general(a, b, (((0,), (0,)), ((), ())), preferred_element_type=F32)


def place(s, y, x, c):
    return {
        "section": lax.rem(s + 8, 8),
        "seq": lax.rem(y + 4, 4) * 4 + lax.rem(x + 4, 4),
        "head": lax.rem(c, 2),
    }


def kernel(
    feat, step, dec, map_in, map_out, seg, grad,
    gf_out, gs_out, gd_out, PM,
    XT, XW, GRN, GRT, GHW, MAP, STEP, DEC, SEG, PREV,
    L, LT, HW, TW, STW, DB, CF, CB, CM, MASK, PRE,
    PF, PB, VI, WS, CK, RK, U, V, B4,
    RF, RB, ES, GS, EA, GA, EB, COF, COB, RDEC, ROWD,
    GIM, GOM, PMS, PX, PO, GF, GSS, GDS, SEGI, SEGF, RAW, MAPS, MAPT,
    ssem, rs_one, ss_grad, rs_feat, rs_grad, rs_f, rs_b, ready,
):
    s = lax.axis_index("section")
    q = lax.axis_index("seq")
    c = lax.axis_index("head")
    y = q // 4
    x = lax.rem(q, 4)
    co = x // 2
    half = lax.rem(x, 2)
    first_head = 32 * half + 16 * c
    R_SEG, R_STEP, R_DEC, R_MAP, R_PREV, R_GF, R_GS, R_GD, R_PM, R_RD, R_A, R_B, R_C, R_CROSS, R_SUM = range(15)

    barrier = pltpu.get_barrier_semaphore()
    load_seg = pltpu.make_async_copy(seg, SEGI, rs_one.at[R_A])
    load_in = pltpu.make_async_copy(map_in, RAW.at[0], rs_one.at[R_B])
    load_out = pltpu.make_async_copy(map_out, RAW.at[1], rs_one.at[R_C])
    load_seg.start()
    load_in.start()
    load_out.start()

    def greet(target):
        pl.semaphore_signal(barrier, inc=1, device_id=target, device_id_type=MESH)

    for dx in range(1, 4):
        greet(place(s, y, x + dx, 0))

    @pl.when(c == 1)
    def _():
        greet(place(s, y, x, 0))

    for dx in range(4):
        greet(place(s + 1, y, x + dx, 1))
    for dy in range(1, 4):
        greet(place(s, y + dy, x, 1))

    load_seg.wait()
    SEGF[...] = jnp.broadcast_to(SEGI[...].astype(F32), (8, T))
    load_in.wait()
    load_out.wait()
    for g in range(2):
        MAPS[g, 0] = RAW[0, :, g, :]
        MAPS[g, 1] = RAW[1, :, g, :]

    @pl.when(c == 0)
    def _():
        pl.semaphore_wait(barrier, 7)
        pl.semaphore_signal(ready, inc=1, device_id=place(s, y, x, 1), device_id_type=MESH)

    @pl.when(c == 1)
    def _():
        pl.semaphore_wait(ready, 1)

    pending = []
    count = itertools.count()

    def send(src, dst, rsem, target, own=None):
        copy = pltpu.make_async_remote_copy(
            src_ref=src, dst_ref=dst, send_sem=ssem.at[next(count)], recv_sem=rsem,
            device_id=target, device_id_type=MESH,
        )
        if own is None:
            copy.start()
            pending.append((None, copy))
        else:
            away = jnp.logical_not(own)

            @pl.when(own)
            def _():
                pltpu.make_async_copy(src, dst, rsem).start()

            @pl.when(away)
            def _():
                copy.start()

            pending.append((away, copy))

    def sent(sends):
        for away, copy in sends:
            if away is None:
                copy.wait_send()
            else:
                @pl.when(away)
                def _(copy=copy):
                    copy.wait_send()

    def arrived(ref, sem):
        pltpu.make_async_copy(ref, ref, sem).wait()

    pltpu.make_async_copy(SEGF, SEG.at[x], rs_one.at[R_SEG]).start()
    for dx in range(1, 4):
        send(SEGF, SEG.at[x], rs_one.at[R_SEG], place(s, y, x + dx, c))
    chips = [lax.rem(x + dx, 4) for dx in range(4)]
    workers = []
    for gl in range(2):
        for dc in range(2):
            xw = 2 * c + gl
            own = (xw == x) if dc == 0 else None
            workers.append((gl, xw, lax.rem(c + dc, 2), own))

    def to_owner(src, dst, rsem, dx):
        own = (c == co) if dx == 0 else None
        send(src, dst, rsem, place(s, y, chips[dx], co), own)

    for gl, xw, cw, own in workers:
        rows = pl.ds(pl.multiple_of(32 * gl + 16 * cw, 16), 16)
        send(step.at[rows], STEP.at[x], rs_one.at[R_STEP], place(s, y, xw, cw), own)
        send(dec.at[rows], DEC.at[x], rs_one.at[R_DEC], place(s, y, xw, cw), own)
    for gl, xw, cw, own in workers:
        send(MAPS.at[gl, cw], MAP.at[cw, x], rs_one.at[R_MAP], place(s, y, xw, cw), own)
    feat_sends = {}

    def issue_feat(k):
        before = len(pending)
        for gl, xw, cw, own in workers:
            rows = pl.ds(pl.multiple_of((32 * gl + 16 * cw + HC * k) * W, CW), CW)
            send(feat.at[rows], XT.at[k, x], rs_feat.at[k], place(s, y, xw, cw), own)
        feat_sends[k] = pending[before:]
        del pending[before:]

    def issue_grad(k):
        for dx in range(4):
            for dc in range(2):
                xw = lax.rem(x + dx, 4)
                cw = lax.rem(c + dc, 2)
                cols = pl.ds(pl.multiple_of((32 * xw + 16 * cw + HC * k) * W, CW), CW)
                pltpu.make_async_remote_copy(
                    src_ref=grad.at[:, cols],
                    dst_ref=GRN.at[k, x, pl.ds(pl.multiple_of(64 * c, 64), 64), :],
                    send_sem=ss_grad.at[k],
                    recv_sem=rs_grad.at[k],
                    device_id=place(s - 1, y, xw, cw),
                    device_id_type=MESH,
                ).start()

    def gone(k):
        sent(feat_sends[k])
        arrived(grad.at[:, pl.ds(0, 8 * CW)], ss_grad.at[k])

    for k in range(WINDOW):
        issue_feat(k)

    @pl.when(c == 1)
    def _():
        pl.semaphore_wait(barrier, 14)
        pl.semaphore_signal(ready, inc=1, device_id=place(s, y, x, 0), device_id_type=MESH)

    @pl.when(c == 0)
    def _():
        pl.semaphore_wait(ready, 1)

    for k in range(WINDOW):
        issue_grad(k)

    arrived(SEG, rs_one.at[R_SEG])
    send(SEG.at[3], PREV, rs_one.at[R_PREV], place(s, y + 1, x, c))
    arrived(STEP, rs_one.at[R_STEP])
    arrived(DEC, rs_one.at[R_DEC])
    row_id = lax.broadcasted_iota(jnp.int32, (T, T), 0)
    col_id = lax.broadcasted_iota(jnp.int32, (T, T), 1)
    upper = (row_id <= col_id).astype(F32)
    for b in range(ROW):
        total = dot(DEC[b], upper, HIGHEST)
        L[b] = total
        padded = jnp.concatenate([total, jnp.zeros((T - HEADS, T), F32)], axis=0)
        LT[b] = jnp.transpose(padded)
        seg_row = SEG[b][0:1, :]
        seg_col = jnp.transpose(jnp.broadcast_to(seg_row, (T, T)))
        same = (seg_col == seg_row).astype(F32)
        MASK[b] = jnp.where(row_id >= col_id, same, 0.0)
        PRE[b] = jnp.where(row_id < col_id, same, 0.0)
    arrived(PREV, rs_one.at[R_PREV])
    first = (y > 0).astype(F32)
    decays = []
    for b in range(ROW):
        total = L[b]
        seg_row = SEG[b][0:1, :]
        if b == 0:
            previous = PREV[0:1, T - 1 : T] * first
        else:
            previous = SEG[b - 1][0:1, T - 1 : T]
        last = total[:, T - 1 : T]
        seg_last = seg_row[:, T - 1 : T]
        carried = (seg_row == previous).astype(F32)
        tail = (seg_row == seg_last).astype(F32)
        HW[b] = carried * jnp.exp(total)
        tw = tail * jnp.exp(last - total)
        TW[b] = tw
        STW[b] = STEP[b] * tw
        d = jnp.broadcast_to((seg_last == previous).astype(F32) * jnp.exp(last), (HEADS, N))
        DB[b] = d
        decays.append(d)
    one = jnp.ones((HEADS, N), F32)
    run = one
    for b in range(ROW):
        CF[b] = run
        run = run * decays[b]
    CF[ROW] = run
    run = one
    for b in reversed(range(ROW)):
        CB[b] = run
        run = run * decays[b]
    ROWD[...] = CF[ROW][:, 0:T]
    pltpu.make_async_copy(ROWD, RDEC.at[y], rs_one.at[R_RD]).start()
    for dy in range(1, 4):
        send(ROWD, RDEC.at[y], rs_one.at[R_RD], place(s, y + dy, x, c))
    arrived(MAP.at[c], rs_one.at[R_MAP])
    send(MAP.at[c], MAP.at[c], rs_one.at[R_CROSS], place(s, y, x, c + 1))
    arrived(MAP.at[1 - c], rs_one.at[R_CROSS])
    for b in range(ROW):
        MAPT[b, 0] = jnp.transpose(MAP[0, b])
        MAPT[b, 1] = jnp.transpose(MAP[1, b])
        CM[b] = dot(MAP[1, b], MAPT[b, 0])
        WS[b] = jnp.zeros((T, T), F32)
        RK[b] = jnp.zeros((T, T), F32)
        GIM[b] = jnp.zeros((T, N), F32)
        GOM[b] = jnp.zeros((T, N), F32)

    def by_head(a):
        return a.reshape(HC, W, a.shape[-1])

    def scaled(a, w):
        return (by_head(a) * w[:, None, :]).reshape(a.shape)

    def heads_of(ref, b, k):
        return ref[b, HC * k : HC * (k + 1), :]

    def copy_f(k, to):
        return pltpu.make_async_remote_copy(
            src_ref=ES.at[k], dst_ref=RF.at[k, y], send_sem=ssem.at[FBASE + 6 * k + to - 1],
            recv_sem=rs_f.at[k, y], device_id=place(s, to, x, c), device_id_type=MESH,
        )

    def copy_b(k, to):
        return pltpu.make_async_remote_copy(
            src_ref=GS.at[k], dst_ref=RB.at[k, y - 1], send_sem=ssem.at[FBASE + 6 * k + 3 + to],
            recv_sem=rs_b.at[k, y - 1], device_id=place(s, to, x, c), device_id_type=MESH,
        )

    def local_states(k):
        arrived(XT.at[k], rs_feat.at[k])
        total = jnp.zeros((CW, N), F32)
        PF[k, 0] = total
        for b in range(ROW):
            xw = scaled(XT[k, b].astype(F32), heads_of(STW, b, k)).astype(BF16)
            XW[k, b] = xw
            total = scaled(total, heads_of(DB, b, k)) + dot(xw, MAP[0, b])
            PF[k, b + 1] = total
        ES[k] = total.astype(BF16)
        for to in range(1, 4):
            @pl.when(y < to)
            def _(to=to):
                copy_f(k, to).start()

    def local_grads(k):
        arrived(GRN.at[k], rs_grad.at[k])
        total = jnp.zeros((CW, N), F32)
        PB[k, ROW] = total
        for b in reversed(range(ROW)):
            gt = jnp.transpose(GRN[k, b])
            GRT[k, b] = gt
            gh = scaled(gt.astype(F32), heads_of(HW, b, k)).astype(BF16)
            GHW[k, b] = gh
            total = scaled(total, heads_of(DB, b, k)) + dot(gh, MAP[1, b])
            PB[k, b] = total
        GS[k] = total.astype(BF16)
        for to in range(3):
            @pl.when(y > to)
            def _(to=to):
                copy_b(k, to).start()

    def enter_f(k):
        EA[...] = jnp.zeros((CW, N), F32)
        for src in range(3):
            @pl.when(y > src)
            def _(src=src):
                arrived(RF.at[k, src], rs_f.at[k, src])
                coef = COF[src, HC * k : HC * (k + 1), :]
                EA[...] += scaled(RF[k, src].astype(F32), coef)

    def enter_b(k):
        GA[...] = jnp.zeros((CW, N), F32)
        for src in range(1, 4):
            @pl.when(y < src)
            def _(src=src):
                arrived(RB.at[k, src - 1], rs_b.at[k, src - 1])
                coef = COB[src - 1, HC * k : HC * (k + 1), :]
                GA[...] += scaled(RB[k, src - 1].astype(F32), coef)

    def intra(k):
        def one_block(b, carry):
            xt = XT[k, b]
            zero = jnp.zeros((W, T), BF16)
            spread = jnp.concatenate(
                [
                    jnp.concatenate(
                        [xt[W * h : W * (h + 1)] if h == j else zero for j in range(HC)], axis=1
                    )
                    for h in range(HC)
                ],
                axis=0,
            )
            pairs = dot(GRN[k, b], spread)
            mask = MASK[b] > 0.0
            cross = CM[b]
            columns = LT[b]
            held = WS[b]
            sums = RK[b]
            lane = lax.broadcasted_iota(jnp.int32, (T, T), 1)
            cols = []
            for h in range(HC):
                head = HC * k + h
                gap = columns[:, head : head + 1] - L[b, head : head + 1, :]
                m = jnp.where(mask, jnp.exp(gap), 0.0)
                a = (m * cross).astype(BF16)
                VI[k, b, W * h : W * (h + 1), :] = dot(GRT[k, b, W * h : W * (h + 1), :], a)
                wh = m * pairs[:, T * h : T * (h + 1)] * STEP[b, head : head + 1, :]
                held = held + wh
                kk = wh * cross
                cols.append(jnp.sum(kk, axis=0, keepdims=True))
                sums = jnp.where(lane == head, jnp.sum(kk, axis=1, keepdims=True), sums)
            CK[b, HC * k : HC * (k + 1), :] = jnp.concatenate(cols, axis=0)
            WS[b] = held
            RK[b] = sums
            return carry

        lax.fori_loop(0, ROW, one_block, 0, unroll=4)

    def row_factors():
        arrived(RDEC, rs_one.at[R_RD])
        one = jnp.ones((HEADS, T), F32)
        for src in range(3):
            coef = one
            for r in range(src + 1, 3):
                coef = coef * jnp.where(y > r, RDEC[r], one)
            COF[src] = jnp.concatenate([coef, coef], axis=1)
            coef = one
            for r in range(1, src + 1):
                coef = coef * jnp.where(y < r, RDEC[r], one)
            COB[src] = jnp.concatenate([coef, coef], axis=1)

    def finish_f(k):
        enter_f(k)

        def one_block(b, carry):
            eb = (PF[k, b] + scaled(EA[...], heads_of(CF, b, k))).astype(BF16)
            EB[k, b] = eb
            seen = dot(eb, MAPT[b, 1])
            hs = slice(HC * k, HC * (k + 1))
            U[b, hs, :] = heads_of(HW, b, k) * jnp.sum(by_head(GRT[k, b].astype(F32) * seen), axis=1)
            GOM[b] += dot_tn(GHW[k, b], eb)
            return carry

        lax.fori_loop(0, ROW, one_block, 0, unroll=4)

    def finish_b(k):
        enter_b(k)

        def one_block(b, carry):
            gb = (PB[k, b + 1] + scaled(GA[...], heads_of(CB, b, k))).astype(BF16)
            lift = dot(gb, MAPT[b, 0])
            val = VI[k, b] + scaled(lift, heads_of(TW, b, k))
            GF[k, b] = scaled(val, heads_of(STEP, b, k)).astype(BF16)
            hs = slice(HC * k, HC * (k + 1))
            V[b, hs, :] = heads_of(STW, b, k) * jnp.sum(by_head(XT[k, b].astype(F32) * lift), axis=1)
            both = jnp.sum(by_head(EB[k, b].astype(F32) * gb.astype(F32)), axis=1)
            B4[b, hs, :] = jnp.broadcast_to(jnp.sum(both, axis=1, keepdims=True), (HC, T))
            GIM[b] += dot_tn(XW[k, b], gb)
            return carry

        lax.fori_loop(0, ROW, one_block, 0, unroll=4)
        for dx in range(4):
            rows = pl.ds(pl.multiple_of((first_head + HC * k) * W, CW), CW)
            to_owner(GF.at[k, chips[dx]], gf_out.at[rows], rs_one.at[R_GF], dx)

    def send_map(m, first, second):
        @pl.when(c != m)
        def _():
            for b in range(ROW):
                PMS[b] = (first[b] + second(b)).astype(BF16)
            cross[m].start()

        @pl.when(c == m)
        def _():
            for b in range(ROW):
                first[b] = first[b] + second(b)
            arrived(PX, rs_one.at[R_SUM])
            for b in range(ROW):
                PO[b] = (first[b] + PX[b].astype(F32)).astype(BF16)
            for dx in range(4):
                if dx == 0:
                    @pl.when(c == co)
                    def _():
                        pltpu.make_async_copy(PO.at[x], PM.at[half, m], rs_one.at[R_PM]).start()

                    @pl.when(c != co)
                    def _():
                        summed[m][0].start()
                else:
                    summed[m][dx].start()

    cross, summed = [], []
    for m in range(2):
        cross.append(
            pltpu.make_async_remote_copy(
                src_ref=PMS, dst_ref=PX, send_sem=ssem.at[next(count)], recv_sem=rs_one.at[R_SUM],
                device_id=place(s, y, x, c + 1), device_id_type=MESH,
            )
        )
        pending.append((c != m, cross[m]))
        summed.append([])
        for dx in range(4):
            summed[m].append(
                pltpu.make_async_remote_copy(
                    src_ref=PO.at[chips[dx]], dst_ref=PM.at[half, m], send_sem=ssem.at[next(count)],
                    recv_sem=rs_one.at[R_PM], device_id=place(s, y, chips[dx], co),
                    device_id_type=MESH,
                )
            )
            going = c == m
            if dx == 0:
                going = jnp.logical_and(going, c != co)
            pending.append((going, summed[m][dx]))

    for k in range(CHUNKS):
        local_states(k)
        local_grads(k)
        gone(k)
        if k + WINDOW < CHUNKS:
            issue_feat(k + WINDOW)
            issue_grad(k + WINDOW)
        intra(k)
        if k == 0:
            row_factors()
        if k >= LAG:
            finish_f(k - LAG)
            finish_b(k - LAG)
    for k in range(CHUNKS - LAG, CHUNKS):
        finish_f(k)
        if k + 1 == CHUNKS:
            send_map(1, GOM, lambda b: dot(WS[b].astype(BF16), MAP[0, b]))
        finish_b(k)
    send_map(0, GIM, lambda b: dot_tn(WS[b].astype(BF16), MAP[1, b]))

    for b in range(ROW):
        row_sums = jnp.transpose(RK[b])[0:HEADS, :]
        ck = CK[b]
        v = V[b]
        GSS[b] = (ck + v) / STEP[b]
        chain = dot(row_sums - ck + U[b], MASK[b], HIGHEST) + dot(v, PRE[b], HIGHEST)
        GDS[b] = chain + HW[b] * TW[b] * B4[b]
    for dx in range(4):
        rows = pl.ds(pl.multiple_of(first_head, 16), 16)
        to_owner(GSS.at[chips[dx]], gs_out.at[rows], rs_one.at[R_GS], dx)
        to_owner(GDS.at[chips[dx]], gd_out.at[rows], rs_one.at[R_GD], dx)

    arrived(PM, rs_one.at[R_PM])
    arrived(gf_out, rs_one.at[R_GF])
    arrived(gs_out, rs_one.at[R_GS])
    arrived(gd_out, rs_one.at[R_GD])
    assert next(count) <= FBASE
    sent(pending)
    for k in range(CHUNKS):
        for to in range(1, 4):
            @pl.when(y < to)
            def _():
                copy_f(k, to).wait_send()
        for to in range(3):
            @pl.when(y > to)
            def _():
                copy_b(k, to).wait_send()


def settle(
    gf, gs, gd, pm, gf_out, gs_out, gd_out, gim_out, gom_out,
    held, steps, maps, sums, sem_in, sem_out,
):
    size = 64 * W // PIECES
    reads, writes = [], []
    for g in range(2):
        reads.append(pltpu.make_async_copy(pm.at[g], maps.at[g], sem_in.at[g]))
    for i in range(PIECES):
        rows = pl.ds(i * size, size)
        reads.append(pltpu.make_async_copy(gf.at[rows], held.at[rows], sem_in.at[2 + i]))
        writes.append(pltpu.make_async_copy(held.at[rows], gf_out.at[rows], sem_out.at[i]))
    for i, (a, b) in enumerate(((gs, gs_out), (gd, gd_out))):
        reads.append(pltpu.make_async_copy(a, steps.at[i], sem_in.at[2 + PIECES + i]))
        writes.append(pltpu.make_async_copy(steps.at[i], b, sem_out.at[PIECES + i]))
    for copy in reads:
        copy.start()
    for g in range(2):
        reads[g].wait()
        for m in range(2):
            sums[m, :, g, :] = maps[g, m].astype(F32)
    for m, out in enumerate((gim_out, gom_out)):
        copy = pltpu.make_async_copy(sums.at[m], out, sem_out.at[PIECES + 2 + m])
        copy.start()
        writes.append(copy)
    for i in range(PIECES + 2):
        reads[2 + i].wait()
        writes[i].start()
    for copy in writes:
        copy.wait()


def per_device(features, step_size, log_decay, input_map, output_map, segment, sent_grad):
    feat = jnp.transpose(features[0], (1, 2, 0)).reshape(64 * W, T)
    step = step_size[0].T
    dec = log_decay[0].T
    grad = sent_grad[0]
    any_ = pl.BlockSpec(memory_space=pltpu.HBM)
    V_ = pltpu.VMEM
    scratch = [
        V_((CHUNKS, ROW, CW, T), BF16),
        V_((CHUNKS, ROW, CW, T), BF16),
        V_((CHUNKS, ROW, T, CW), BF16),
        V_((CHUNKS, ROW, CW, T), BF16),
        V_((CHUNKS, ROW, CW, T), BF16),
        V_((2, ROW, T, N), BF16),
        V_((ROW, HEADS, T), F32),
        V_((ROW, HEADS, T), F32),
        V_((ROW, 8, T), F32),
        V_((8, T), F32),
        V_((ROW, HEADS, T), F32),
        V_((ROW, T, T), F32),
        V_((ROW, HEADS, T), F32),
        V_((ROW, HEADS, T), F32),
        V_((ROW, HEADS, T), F32),
        V_((ROW, HEADS, N), F32),
        V_((ROW + 1, HEADS, N), F32),
        V_((ROW, HEADS, N), F32),
        V_((ROW, T, T), F32),
        V_((ROW, T, T), F32),
        V_((ROW, T, T), F32),
        V_((CHUNKS, ROW + 1, CW, N), F32),
        V_((CHUNKS, ROW + 1, CW, N), F32),
        V_((CHUNKS, ROW, CW, T), F32),
        V_((ROW, T, T), F32),
        V_((ROW, HEADS, T), F32),
        V_((ROW, T, T), F32),
        V_((ROW, HEADS, T), F32),
        V_((ROW, HEADS, T), F32),
        V_((ROW, HEADS, T), F32),
        V_((CHUNKS, 3, CW, N), BF16),
        V_((CHUNKS, 3, CW, N), BF16),
        V_((CHUNKS, CW, N), BF16),
        V_((CHUNKS, CW, N), BF16),
        V_((CW, N), F32),
        V_((CW, N), F32),
        V_((CHUNKS, ROW, CW, N), BF16),
        V_((3, HEADS, N), F32),
        V_((3, HEADS, N), F32),
        V_((4, HEADS, T), F32),
        V_((HEADS, T), F32),
        V_((ROW, T, N), F32),
        V_((ROW, T, N), F32),
        V_((ROW, T, N), BF16),
        V_((ROW, T, N), BF16),
        V_((ROW, T, N), BF16),
        V_((CHUNKS, ROW, CW, T), BF16),
        V_((ROW, HEADS, T), F32),
        V_((ROW, HEADS, T), F32),
        V_((1, T), jnp.int32),
        V_((8, T), F32),
        V_((2, T, 2, N), BF16),
        V_((2, 2, T, N), BF16),
        V_((ROW, 2, N, T), BF16),
        pltpu.SemaphoreType.DMA((FBASE + 6 * CHUNKS,)),
        pltpu.SemaphoreType.DMA((15,)),
        pltpu.SemaphoreType.DMA((CHUNKS,)),
        pltpu.SemaphoreType.DMA((CHUNKS,)),
        pltpu.SemaphoreType.DMA((CHUNKS,)),
        pltpu.SemaphoreType.DMA((CHUNKS, 3)),
        pltpu.SemaphoreType.DMA((CHUNKS, 3)),
        pltpu.SemaphoreType.REGULAR,
    ]
    gf, gs, gd, pm = pl.pallas_call(
        kernel,
        out_shape=(
            jax.ShapeDtypeStruct((64 * W, T), BF16),
            jax.ShapeDtypeStruct((64, T), F32),
            jax.ShapeDtypeStruct((64, T), F32),
            jax.ShapeDtypeStruct((2, 2, T, N), BF16),
        ),
        in_specs=[any_] * 7,
        out_specs=(any_, any_, any_, any_),
        scratch_shapes=scratch,
        compiler_params=pltpu.CompilerParams(
            collective_id=0, has_side_effects=True, vmem_limit_bytes=60 * 2**20
        ),
        name="ssd_backward",
    )(feat, step, dec, input_map[0], output_map[0], segment, grad)
    gf, gs, gd, gim, gom = pl.pallas_call(
        settle,
        out_shape=(
            jax.ShapeDtypeStruct((64 * W, T), BF16),
            jax.ShapeDtypeStruct((64, T), F32),
            jax.ShapeDtypeStruct((64, T), F32),
            jax.ShapeDtypeStruct((T, 2, N), F32),
            jax.ShapeDtypeStruct((T, 2, N), F32),
        ),
        in_specs=[any_] * 4,
        out_specs=(any_,) * 5,
        scratch_shapes=[
            V_((64 * W, T), BF16),
            V_((2, 64, T), F32),
            V_((2, 2, T, N), BF16),
            V_((2, T, 2, N), F32),
            pltpu.SemaphoreType.DMA((PIECES + 4,)),
            pltpu.SemaphoreType.DMA((PIECES + 4,)),
        ],
        compiler_params=pltpu.CompilerParams(vmem_limit_bytes=60 * 2**20),
        name="settle",
    )(gf, gs, gd, pm)
    return (
        jnp.transpose(gf.reshape(64, W, T), (2, 0, 1))[None],
        gs.T[None],
        gd.T[None],
        gim[None],
        gom[None],
    )


def solution(mesh):
    placed = (
        P("section", "seq", "head", None),
        P("section", "seq", "head"),
        P("section", "seq", "head"),
        P("section", "seq", "head", None),
        P("section", "seq", "head", None),
        P("section", "seq"),
        P("section", ("seq", "head"), None),
    )
    return jax.shard_map(
        per_device,
        mesh=mesh,
        in_specs=placed,
        out_specs=(
            P("section", "seq", "head", None),
            P("section", "seq", "head"),
            P("section", "seq", "head"),
            P("section", "seq", "head", None),
            P("section", "seq", "head", None),
        ),
        check_vma=False,
    )
```

```python
import itertools

import jax
import jax.numpy as jnp
from jax import lax
from jax.experimental import pallas as pl
from jax.experimental.pallas import tpu as pltpu
from jax.sharding import PartitionSpec as P

MESH = pl.DeviceIdType.MESH
F32 = jnp.float32
BF16 = jnp.bfloat16
HIGHEST = lax.Precision.HIGHEST

T = 128
W = 64
N = 256
ROW = 4
HEADS = 16
CHUNKS = 8
HC = HEADS // CHUNKS
WINDOW = 4
PIECES = 4
LAG = 3
CW = HC * W
FBASE = 48 + 8 * CHUNKS


def dot(a, b, precision=None):
    return lax.dot_general(
        a, b, (((1,), (0,)), ((), ())), precision=precision, preferred_element_type=F32
    )


def dot_nt(a, b, precision=None):
    return lax.dot_general(
        a, b, (((1,), (1,)), ((), ())), precision=precision, preferred_element_type=F32
    )


def dot_tn(a, b):
    return lax.dot_general(a, b, (((0,), (0,)), ((), ())), preferred_element_type=F32)


def place(s, y, x, c):
    return {
        "section": lax.rem(s + 8, 8),
        "seq": lax.rem(y + 4, 4) * 4 + lax.rem(x + 4, 4),
        "head": lax.rem(c, 2),
    }


def kernel(
    feat, step, dec, map_in, map_out, seg, grad,
    gf_out, gs_out, gd_out, PM,
    XT, XW, GRN, GRT, GHW, MAP, STEP, DEC, SEG, PREV,
    L, LT, HW, TW, STW, DB, CF, CB, CM, MASK, PRE,
    PF, PB, VI, WS, CK, RK, U, V, B4,
    RF, RB, ES, GS, EA, GA, EB, COF, COB, RDEC, ROWD,
    GIM, GOM, PMS, PX, PO, GF, GSS, GDS, SEGI, SEGF, RAW, MAPS, MAPT,
    ssem, rs_one, ss_grad, rs_feat, rs_grad, rs_f, rs_b, ready,
):
    s = lax.axis_index("section")
    q = lax.axis_index("seq")
    c = lax.axis_index("head")
    y = q // 4
    x = lax.rem(q, 4)
    co = x // 2
    half = lax.rem(x, 2)
    first_head = 32 * half + 16 * c
    R_SEG, R_STEP, R_DEC, R_MAP, R_PREV, R_GF, R_GS, R_GD, R_PM, R_RD, R_A, R_B, R_C, R_CROSS, R_SUM = range(15)

    barrier = pltpu.get_barrier_semaphore()
    load_seg = pltpu.make_async_copy(seg, SEGI, rs_one.at[R_A])
    load_in = pltpu.make_async_copy(map_in, RAW.at[0], rs_one.at[R_B])
    load_out = pltpu.make_async_copy(map_out, RAW.at[1], rs_one.at[R_C])
    load_seg.start()
    load_in.start()
    load_out.start()

    def greet(target):
        pl.semaphore_signal(barrier, inc=1, device_id=target, device_id_type=MESH)

    for dx in range(1, 4):
        greet(place(s, y, x + dx, 0))

    @pl.when(c == 1)
    def _():
        greet(place(s, y, x, 0))

    for dx in range(4):
        greet(place(s + 1, y, x + dx, 1))
    for dy in range(1, 4):
        greet(place(s, y + dy, x, 1))

    load_seg.wait()
    SEGF[...] = jnp.broadcast_to(SEGI[...].astype(F32), (8, T))
    load_in.wait()
    load_out.wait()
    for g in range(2):
        MAPS[g, 0] = RAW[0, :, g, :]
        MAPS[g, 1] = RAW[1, :, g, :]

    @pl.when(c == 0)
    def _():
        pl.semaphore_wait(barrier, 7)
        pl.semaphore_signal(ready, inc=1, device_id=place(s, y, x, 1), device_id_type=MESH)

    @pl.when(c == 1)
    def _():
        pl.semaphore_wait(ready, 1)

    pending = []
    count = itertools.count()

    def send(src, dst, rsem, target, own=None):
        copy = pltpu.make_async_remote_copy(
            src_ref=src, dst_ref=dst, send_sem=ssem.at[next(count)], recv_sem=rsem,
            device_id=target, device_id_type=MESH,
        )
        if own is None:
            copy.start()
            pending.append((None, copy))
        else:
            away = jnp.logical_not(own)

            @pl.when(own)
            def _():
                pltpu.make_async_copy(src, dst, rsem).start()

            @pl.when(away)
            def _():
                copy.start()

            pending.append((away, copy))

    def sent(sends):
        for away, copy in sends:
            if away is None:
                copy.wait_send()
            else:
                @pl.when(away)
                def _(copy=copy):
                    copy.wait_send()

    def arrived(ref, sem):
        pltpu.make_async_copy(ref, ref, sem).wait()

    pltpu.make_async_copy(SEGF, SEG.at[x], rs_one.at[R_SEG]).start()
    for dx in range(1, 4):
        send(SEGF, SEG.at[x], rs_one.at[R_SEG], place(s, y, x + dx, c))
    chips = [lax.rem(x + dx, 4) for dx in range(4)]
    workers = []
    for gl in range(2):
        for dc in range(2):
            xw = 2 * c + gl
            own = (xw == x) if dc == 0 else None
            workers.append((gl, xw, lax.rem(c + dc, 2), own))

    def to_owner(src, dst, rsem, dx):
        own = (c == co) if dx == 0 else None
        send(src, dst, rsem, place(s, y, chips[dx], co), own)

    for gl, xw, cw, own in workers:
        rows = pl.ds(pl.multiple_of(32 * gl + 16 * cw, 16), 16)
        send(step.at[rows], STEP.at[x], rs_one.at[R_STEP], place(s, y, xw, cw), own)
        send(dec.at[rows], DEC.at[x], rs_one.at[R_DEC], place(s, y, xw, cw), own)
    for gl, xw, cw, own in workers:
        send(MAPS.at[gl, cw], MAP.at[cw, x], rs_one.at[R_MAP], place(s, y, xw, cw), own)
    feat_sends = {}

    def issue_feat(k):
        before = len(pending)
        for gl, xw, cw, own in workers:
            rows = pl.ds(pl.multiple_of((32 * gl + 16 * cw + HC * k) * W, CW), CW)
            send(feat.at[rows], XT.at[k, x], rs_feat.at[k], place(s, y, xw, cw), own)
        feat_sends[k] = pending[before:]
        del pending[before:]

    def issue_grad(k):
        for dx in range(4):
            for dc in range(2):
                xw = lax.rem(x + dx, 4)
                cw = lax.rem(c + dc, 2)
                cols = pl.ds(pl.multiple_of((32 * xw + 16 * cw + HC * k) * W, CW), CW)
                pltpu.make_async_remote_copy(
                    src_ref=grad.at[:, cols],
                    dst_ref=GRN.at[k, x, pl.ds(pl.multiple_of(64 * c, 64), 64), :],
                    send_sem=ss_grad.at[k],
                    recv_sem=rs_grad.at[k],
                    device_id=place(s - 1, y, xw, cw),
                    device_id_type=MESH,
                ).start()

    def gone(k):
        sent(feat_sends[k])
        arrived(grad.at[:, pl.ds(0, 8 * CW)], ss_grad.at[k])

    for k in range(WINDOW):
        issue_feat(k)

    @pl.when(c == 1)
    def _():
        pl.semaphore_wait(barrier, 14)
        pl.semaphore_signal(ready, inc=1, device_id=place(s, y, x, 0), device_id_type=MESH)

    @pl.when(c == 0)
    def _():
        pl.semaphore_wait(ready, 1)

    for k in range(WINDOW):
        issue_grad(k)

    arrived(SEG, rs_one.at[R_SEG])
    send(SEG.at[3], PREV, rs_one.at[R_PREV], place(s, y + 1, x, c))
    arrived(STEP, rs_one.at[R_STEP])
    arrived(DEC, rs_one.at[R_DEC])
    row_id = lax.broadcasted_iota(jnp.int32, (T, T), 0)
    col_id = lax.broadcasted_iota(jnp.int32, (T, T), 1)
    upper = (row_id <= col_id).astype(F32)
    for b in range(ROW):
        total = dot(DEC[b], upper, HIGHEST)
        L[b] = total
        padded = jnp.concatenate([total, jnp.zeros((T - HEADS, T), F32)], axis=0)
        LT[b] = jnp.transpose(padded)
        seg_row = SEG[b][0:1, :]
        seg_col = jnp.transpose(jnp.broadcast_to(seg_row, (T, T)))
        same = (seg_col == seg_row).astype(F32)
        MASK[b] = jnp.where(row_id >= col_id, same, 0.0)
        PRE[b] = jnp.where(row_id < col_id, same, 0.0)
    arrived(PREV, rs_one.at[R_PREV])
    first = (y > 0).astype(F32)
    decays = []
    for b in range(ROW):
        total = L[b]
        seg_row = SEG[b][0:1, :]
        if b == 0:
            previous = PREV[0:1, T - 1 : T] * first
        else:
            previous = SEG[b - 1][0:1, T - 1 : T]
        last = total[:, T - 1 : T]
        seg_last = seg_row[:, T - 1 : T]
        carried = (seg_row == previous).astype(F32)
        tail = (seg_row == seg_last).astype(F32)
        HW[b] = carried * jnp.exp(total)
        tw = tail * jnp.exp(last - total)
        TW[b] = tw
        STW[b] = STEP[b] * tw
        d = jnp.broadcast_to((seg_last == previous).astype(F32) * jnp.exp(last), (HEADS, N))
        DB[b] = d
        decays.append(d)
    one = jnp.ones((HEADS, N), F32)
    run = one
    for b in range(ROW):
        CF[b] = run
        run = run * decays[b]
    CF[ROW] = run
    run = one
    for b in reversed(range(ROW)):
        CB[b] = run
        run = run * decays[b]
    ROWD[...] = CF[ROW][:, 0:T]
    pltpu.make_async_copy(ROWD, RDEC.at[y], rs_one.at[R_RD]).start()
    for dy in range(1, 4):
        send(ROWD, RDEC.at[y], rs_one.at[R_RD], place(s, y + dy, x, c))
    arrived(MAP.at[c], rs_one.at[R_MAP])
    send(MAP.at[c], MAP.at[c], rs_one.at[R_CROSS], place(s, y, x, c + 1))
    arrived(MAP.at[1 - c], rs_one.at[R_CROSS])
    for b in range(ROW):
        MAPT[b, 0] = jnp.transpose(MAP[0, b])
        MAPT[b, 1] = jnp.transpose(MAP[1, b])
        CM[b] = dot(MAP[1, b], MAPT[b, 0])
        WS[b] = jnp.zeros((T, T), F32)
        RK[b] = jnp.zeros((T, T), F32)
        GIM[b] = jnp.zeros((T, N), F32)
        GOM[b] = jnp.zeros((T, N), F32)

    def by_head(a):
        return a.reshape(HC, W, a.shape[-1])

    def scaled(a, w):
        return (by_head(a) * w[:, None, :]).reshape(a.shape)

    def heads_of(ref, b, k):
        return ref[b, HC * k : HC * (k + 1), :]

    def copy_f(k, to):
        return pltpu.make_async_remote_copy(
            src_ref=ES.at[k], dst_ref=RF.at[k, y], send_sem=ssem.at[FBASE + 6 * k + to - 1],
            recv_sem=rs_f.at[k, y], device_id=place(s, to, x, c), device_id_type=MESH,
        )

    def copy_b(k, to):
        return pltpu.make_async_remote_copy(
            src_ref=GS.at[k], dst_ref=RB.at[k, y - 1], send_sem=ssem.at[FBASE + 6 * k + 3 + to],
            recv_sem=rs_b.at[k, y - 1], device_id=place(s, to, x, c), device_id_type=MESH,
        )

    def local_states(k):
        arrived(XT.at[k], rs_feat.at[k])
        total = jnp.zeros((CW, N), F32)
        PF[k, 0] = total
        for b in range(ROW):
            xw = scaled(XT[k, b].astype(F32), heads_of(STW, b, k)).astype(BF16)
            XW[k, b] = xw
            total = scaled(total, heads_of(DB, b, k)) + dot(xw, MAP[0, b])
            PF[k, b + 1] = total
        ES[k] = total.astype(BF16)
        for to in range(1, 4):
            @pl.when(y < to)
            def _(to=to):
                copy_f(k, to).start()

    def local_grads(k):
        arrived(GRN.at[k], rs_grad.at[k])
        total = jnp.zeros((CW, N), F32)
        PB[k, ROW] = total
        for b in reversed(range(ROW)):
            gt = jnp.transpose(GRN[k, b])
            GRT[k, b] = gt
            gh = scaled(gt.astype(F32), heads_of(HW, b, k)).astype(BF16)
            GHW[k, b] = gh
            total = scaled(total, heads_of(DB, b, k)) + dot(gh, MAP[1, b])
            PB[k, b] = total
        GS[k] = total.astype(BF16)
        for to in range(3):
            @pl.when(y > to)
            def _(to=to):
                copy_b(k, to).start()

    def enter_f(k):
        EA[...] = jnp.zeros((CW, N), F32)
        for src in range(3):
            @pl.when(y > src)
            def _(src=src):
                arrived(RF.at[k, src], rs_f.at[k, src])
                coef = COF[src, HC * k : HC * (k + 1), :]
                EA[...] += scaled(RF[k, src].astype(F32), coef)

    def enter_b(k):
        GA[...] = jnp.zeros((CW, N), F32)
        for src in range(1, 4):
            @pl.when(y < src)
            def _(src=src):
                arrived(RB.at[k, src - 1], rs_b.at[k, src - 1])
                coef = COB[src - 1, HC * k : HC * (k + 1), :]
                GA[...] += scaled(RB[k, src - 1].astype(F32), coef)

    def intra(k):
        def one_block(b, carry):
            xt = XT[k, b]
            zero = jnp.zeros((W, T), BF16)
            spread = jnp.concatenate(
                [
                    jnp.concatenate(
                        [xt[W * h : W * (h + 1)] if h == j else zero for j in range(HC)], axis=1
                    )
                    for h in range(HC)
                ],
                axis=0,
            )
            pairs = dot(GRN[k, b], spread)
            mask = MASK[b] > 0.0
            cross = CM[b]
            columns = LT[b]
            held = WS[b]
            sums = RK[b]
            lane = lax.broadcasted_iota(jnp.int32, (T, T), 1)
            cols = []
            for h in range(HC):
                head = HC * k + h
                gap = columns[:, head : head + 1] - L[b, head : head + 1, :]
                m = jnp.where(mask, jnp.exp(gap), 0.0)
                a = (m * cross).astype(BF16)
                VI[k, b, W * h : W * (h + 1), :] = dot(GRT[k, b, W * h : W * (h + 1), :], a)
                wh = m * pairs[:, T * h : T * (h + 1)] * STEP[b, head : head + 1, :]
                held = held + wh
                kk = wh * cross
                cols.append(jnp.sum(kk, axis=0, keepdims=True))
                sums = jnp.where(lane == head, jnp.sum(kk, axis=1, keepdims=True), sums)
            CK[b, HC * k : HC * (k + 1), :] = jnp.concatenate(cols, axis=0)
            WS[b] = held
            RK[b] = sums
            return carry

        lax.fori_loop(0, ROW, one_block, 0, unroll=4)

    def row_factors():
        arrived(RDEC, rs_one.at[R_RD])
        one = jnp.ones((HEADS, T), F32)
        for src in range(3):
            coef = one
            for r in range(src + 1, 3):
                coef = coef * jnp.where(y > r, RDEC[r], one)
            COF[src] = jnp.concatenate([coef, coef], axis=1)
            coef = one
            for r in range(1, src + 1):
                coef = coef * jnp.where(y < r, RDEC[r], one)
            COB[src] = jnp.concatenate([coef, coef], axis=1)

    def finish_f(k):
        enter_f(k)

        def one_block(b, carry):
            eb = (PF[k, b] + scaled(EA[...], heads_of(CF, b, k))).astype(BF16)
            EB[k, b] = eb
            seen = dot(eb, MAPT[b, 1])
            hs = slice(HC * k, HC * (k + 1))
            U[b, hs, :] = heads_of(HW, b, k) * jnp.sum(by_head(GRT[k, b].astype(F32) * seen), axis=1)
            GOM[b] += dot_tn(GHW[k, b], eb)
            return carry

        lax.fori_loop(0, ROW, one_block, 0, unroll=4)

    def finish_b(k):
        enter_b(k)

        def one_block(b, carry):
            gb = (PB[k, b + 1] + scaled(GA[...], heads_of(CB, b, k))).astype(BF16)
            lift = dot(gb, MAPT[b, 0])
            val = VI[k, b] + scaled(lift, heads_of(TW, b, k))
            GF[k, b] = scaled(val, heads_of(STEP, b, k)).astype(BF16)
            hs = slice(HC * k, HC * (k + 1))
            V[b, hs, :] = heads_of(STW, b, k) * jnp.sum(by_head(XT[k, b].astype(F32) * lift), axis=1)
            both = jnp.sum(by_head(EB[k, b].astype(F32) * gb.astype(F32)), axis=1)
            B4[b, hs, :] = jnp.broadcast_to(jnp.sum(both, axis=1, keepdims=True), (HC, T))
            GIM[b] += dot_tn(XW[k, b], gb)
            return carry

        lax.fori_loop(0, ROW, one_block, 0, unroll=4)
        for dx in range(4):
            rows = pl.ds(pl.multiple_of((first_head + HC * k) * W, CW), CW)
            to_owner(GF.at[k, chips[dx]], gf_out.at[rows], rs_one.at[R_GF], dx)

    def part_of_map(m, total):
        @pl.when(c != m)
        def _():
            for b in range(ROW):
                PMS[b] = total[b].astype(BF16)
            cross[m].start()

    def sum_of_map(m, total):
        @pl.when(c == m)
        def _():
            arrived(PX, rs_one.at[R_SUM])
            for b in range(ROW):
                PO[b] = (total[b] + PX[b].astype(F32)).astype(BF16)
            for dx in range(4):
                if dx == 0:
                    @pl.when(c == co)
                    def _():
                        pltpu.make_async_copy(PO.at[x], PM.at[half, m], rs_one.at[R_PM]).start()

                    @pl.when(c != co)
                    def _():
                        summed[m][0].start()
                else:
                    summed[m][dx].start()

    cross, summed = [], []
    for m in range(2):
        cross.append(
            pltpu.make_async_remote_copy(
                src_ref=PMS, dst_ref=PX, send_sem=ssem.at[next(count)], recv_sem=rs_one.at[R_SUM],
                device_id=place(s, y, x, c + 1), device_id_type=MESH,
            )
        )
        pending.append((c != m, cross[m]))
        summed.append([])
        for dx in range(4):
            summed[m].append(
                pltpu.make_async_remote_copy(
                    src_ref=PO.at[chips[dx]], dst_ref=PM.at[half, m], send_sem=ssem.at[next(count)],
                    recv_sem=rs_one.at[R_PM], device_id=place(s, y, chips[dx], co),
                    device_id_type=MESH,
                )
            )
            going = c == m
            if dx == 0:
                going = jnp.logical_and(going, c != co)
            pending.append((going, summed[m][dx]))

    for k in range(CHUNKS):
        local_states(k)
        local_grads(k)
        gone(k)
        if k + WINDOW < CHUNKS:
            issue_feat(k + WINDOW)
            issue_grad(k + WINDOW)
        intra(k)
        if k == 0:
            row_factors()
        if k + 1 == CHUNKS:
            for b in range(ROW):
                w = WS[b].astype(BF16)
                GOM[b] += dot(w, MAP[0, b])
                GIM[b] += dot_tn(w, MAP[1, b])
        if k >= LAG:
            finish_f(k - LAG)
            finish_b(k - LAG)
    for k in range(CHUNKS - LAG, CHUNKS):
        finish_f(k)
        if k + 1 == CHUNKS:
            part_of_map(1, GOM)
            for b in range(ROW):
                row_sums = jnp.transpose(RK[b])[0:HEADS, :]
                GDS[b] = dot(row_sums - CK[b] + U[b], MASK[b], HIGHEST)
        finish_b(k)
    part_of_map(0, GIM)
    sum_of_map(0, GIM)
    sum_of_map(1, GOM)

    for b in range(ROW):
        v = V[b]
        GSS[b] = (CK[b] + v) / STEP[b]
        GDS[b] += dot(v, PRE[b], HIGHEST) + HW[b] * TW[b] * B4[b]
    for dx in range(4):
        rows = pl.ds(pl.multiple_of(first_head, 16), 16)
        to_owner(GSS.at[chips[dx]], gs_out.at[rows], rs_one.at[R_GS], dx)
        to_owner(GDS.at[chips[dx]], gd_out.at[rows], rs_one.at[R_GD], dx)

    arrived(PM, rs_one.at[R_PM])
    arrived(gf_out, rs_one.at[R_GF])
    arrived(gs_out, rs_one.at[R_GS])
    arrived(gd_out, rs_one.at[R_GD])
    assert next(count) <= FBASE
    sent(pending)
    for k in range(CHUNKS):
        for to in range(1, 4):
            @pl.when(y < to)
            def _():
                copy_f(k, to).wait_send()
        for to in range(3):
            @pl.when(y > to)
            def _():
                copy_b(k, to).wait_send()


def settle(
    gf, gs, gd, pm, gf_out, gs_out, gd_out, gim_out, gom_out,
    held, steps, maps, sums, sem_in, sem_out,
):
    size = 64 * W // PIECES
    reads, writes = [], []
    for g in range(2):
        reads.append(pltpu.make_async_copy(pm.at[g], maps.at[g], sem_in.at[g]))
    for i in range(PIECES):
        rows = pl.ds(i * size, size)
        reads.append(pltpu.make_async_copy(gf.at[rows], held.at[rows], sem_in.at[2 + i]))
        writes.append(pltpu.make_async_copy(held.at[rows], gf_out.at[rows], sem_out.at[i]))
    for i, (a, b) in enumerate(((gs, gs_out), (gd, gd_out))):
        reads.append(pltpu.make_async_copy(a, steps.at[i], sem_in.at[2 + PIECES + i]))
        writes.append(pltpu.make_async_copy(steps.at[i], b, sem_out.at[PIECES + i]))
    for copy in reads:
        copy.start()
    for g in range(2):
        reads[g].wait()
        for m in range(2):
            sums[m, :, g, :] = maps[g, m].astype(F32)
    for m, out in enumerate((gim_out, gom_out)):
        copy = pltpu.make_async_copy(sums.at[m], out, sem_out.at[PIECES + 2 + m])
        copy.start()
        writes.append(copy)
    for i in range(PIECES + 2):
        reads[2 + i].wait()
        writes[i].start()
    for copy in writes:
        copy.wait()


def per_device(features, step_size, log_decay, input_map, output_map, segment, sent_grad):
    feat = jnp.transpose(features[0], (1, 2, 0)).reshape(64 * W, T)
    step = step_size[0].T
    dec = log_decay[0].T
    grad = sent_grad[0]
    any_ = pl.BlockSpec(memory_space=pltpu.HBM)
    V_ = pltpu.VMEM
    scratch = [
        V_((CHUNKS, ROW, CW, T), BF16),
        V_((CHUNKS, ROW, CW, T), BF16),
        V_((CHUNKS, ROW, T, CW), BF16),
        V_((CHUNKS, ROW, CW, T), BF16),
        V_((CHUNKS, ROW, CW, T), BF16),
        V_((2, ROW, T, N), BF16),
        V_((ROW, HEADS, T), F32),
        V_((ROW, HEADS, T), F32),
        V_((ROW, 8, T), F32),
        V_((8, T), F32),
        V_((ROW, HEADS, T), F32),
        V_((ROW, T, T), F32),
        V_((ROW, HEADS, T), F32),
        V_((ROW, HEADS, T), F32),
        V_((ROW, HEADS, T), F32),
        V_((ROW, HEADS, N), F32),
        V_((ROW + 1, HEADS, N), F32),
        V_((ROW, HEADS, N), F32),
        V_((ROW, T, T), F32),
        V_((ROW, T, T), F32),
        V_((ROW, T, T), F32),
        V_((CHUNKS, ROW + 1, CW, N), F32),
        V_((CHUNKS, ROW + 1, CW, N), F32),
        V_((CHUNKS, ROW, CW, T), F32),
        V_((ROW, T, T), F32),
        V_((ROW, HEADS, T), F32),
        V_((ROW, T, T), F32),
        V_((ROW, HEADS, T), F32),
        V_((ROW, HEADS, T), F32),
        V_((ROW, HEADS, T), F32),
        V_((CHUNKS, 3, CW, N), BF16),
        V_((CHUNKS, 3, CW, N), BF16),
        V_((CHUNKS, CW, N), BF16),
        V_((CHUNKS, CW, N), BF16),
        V_((CW, N), F32),
        V_((CW, N), F32),
        V_((CHUNKS, ROW, CW, N), BF16),
        V_((3, HEADS, N), F32),
        V_((3, HEADS, N), F32),
        V_((4, HEADS, T), F32),
        V_((HEADS, T), F32),
        V_((ROW, T, N), F32),
        V_((ROW, T, N), F32),
        V_((ROW, T, N), BF16),
        V_((ROW, T, N), BF16),
        V_((ROW, T, N), BF16),
        V_((CHUNKS, ROW, CW, T), BF16),
        V_((ROW, HEADS, T), F32),
        V_((ROW, HEADS, T), F32),
        V_((1, T), jnp.int32),
        V_((8, T), F32),
        V_((2, T, 2, N), BF16),
        V_((2, 2, T, N), BF16),
        V_((ROW, 2, N, T), BF16),
        pltpu.SemaphoreType.DMA((FBASE + 6 * CHUNKS,)),
        pltpu.SemaphoreType.DMA((15,)),
        pltpu.SemaphoreType.DMA((CHUNKS,)),
        pltpu.SemaphoreType.DMA((CHUNKS,)),
        pltpu.SemaphoreType.DMA((CHUNKS,)),
        pltpu.SemaphoreType.DMA((CHUNKS, 3)),
        pltpu.SemaphoreType.DMA((CHUNKS, 3)),
        pltpu.SemaphoreType.REGULAR,
    ]
    gf, gs, gd, pm = pl.pallas_call(
        kernel,
        out_shape=(
            jax.ShapeDtypeStruct((64 * W, T), BF16),
            jax.ShapeDtypeStruct((64, T), F32),
            jax.ShapeDtypeStruct((64, T), F32),
            jax.ShapeDtypeStruct((2, 2, T, N), BF16),
        ),
        in_specs=[any_] * 7,
        out_specs=(any_, any_, any_, any_),
        scratch_shapes=scratch,
        compiler_params=pltpu.CompilerParams(
            collective_id=0, has_side_effects=True, vmem_limit_bytes=60 * 2**20
        ),
        name="ssd_backward",
    )(feat, step, dec, input_map[0], output_map[0], segment, grad)
    gf, gs, gd, gim, gom = pl.pallas_call(
        settle,
        out_shape=(
            jax.ShapeDtypeStruct((64 * W, T), BF16),
            jax.ShapeDtypeStruct((64, T), F32),
            jax.ShapeDtypeStruct((64, T), F32),
            jax.ShapeDtypeStruct((T, 2, N), F32),
            jax.ShapeDtypeStruct((T, 2, N), F32),
        ),
        in_specs=[any_] * 4,
        out_specs=(any_,) * 5,
        scratch_shapes=[
            V_((64 * W, T), BF16),
            V_((2, 64, T), F32),
            V_((2, 2, T, N), BF16),
            V_((2, T, 2, N), F32),
            pltpu.SemaphoreType.DMA((PIECES + 4,)),
            pltpu.SemaphoreType.DMA((PIECES + 4,)),
        ],
        compiler_params=pltpu.CompilerParams(vmem_limit_bytes=60 * 2**20),
        name="settle",
    )(gf, gs, gd, pm)
    return (
        jnp.transpose(gf.reshape(64, W, T), (2, 0, 1))[None],
        gs.T[None],
        gd.T[None],
        gim[None],
        gom[None],
    )


def solution(mesh):
    placed = (
        P("section", "seq", "head", None),
        P("section", "seq", "head"),
        P("section", "seq", "head"),
        P("section", "seq", "head", None),
        P("section", "seq", "head", None),
        P("section", "seq"),
        P("section", ("seq", "head"), None),
    )
    return jax.shard_map(
        per_device,
        mesh=mesh,
        in_specs=placed,
        out_specs=(
            P("section", "seq", "head", None),
            P("section", "seq", "head"),
            P("section", "seq", "head"),
            P("section", "seq", "head", None),
            P("section", "seq", "head", None),
        ),
        check_vma=False,
    )
```

```python
import itertools

import jax
import jax.numpy as jnp
from jax import lax
from jax.experimental import pallas as pl
from jax.experimental.pallas import tpu as pltpu
from jax.sharding import PartitionSpec as P

MESH = pl.DeviceIdType.MESH
F32 = jnp.float32
BF16 = jnp.bfloat16
HIGHEST = lax.Precision.HIGHEST

T = 128
W = 64
N = 256
ROW = 4
HEADS = 16
CHUNKS = 8
HC = HEADS // CHUNKS
WINDOW = 4
PIECES = 4
LAG = 3
CW = HC * W
FBASE = 48 + 8 * CHUNKS


def dot(a, b, precision=None):
    return lax.dot_general(
        a, b, (((1,), (0,)), ((), ())), precision=precision, preferred_element_type=F32
    )


def dot_nt(a, b, precision=None):
    return lax.dot_general(
        a, b, (((1,), (1,)), ((), ())), precision=precision, preferred_element_type=F32
    )


def dot_tn(a, b):
    return lax.dot_general(a, b, (((0,), (0,)), ((), ())), preferred_element_type=F32)


def place(s, y, x, c):
    return {
        "section": lax.rem(s + 8, 8),
        "seq": lax.rem(y + 4, 4) * 4 + lax.rem(x + 4, 4),
        "head": lax.rem(c, 2),
    }


def kernel(
    feat, step, dec, map_in, map_out, seg, grad,
    gf_out, gs_out, gd_out, PM,
    XT, XW, GRN, GRT, GHW, MAP, STEP, DEC, SEG, PREV,
    L, LT, HW, TW, STW, DB, CF, CB, CM, MASK, PRE,
    PF, PB, VI, WS, CK, RK, U, V, B4,
    RF, RB, ES, GS, EA, GA, EB, COF, COB, RDEC, ROWD,
    GIM, GOM, PMS, PX, PO, GF, GSS, GDS, SEGI, SEGF, RAW, MAPS, MAPT,
    ssem, rs_one, ss_grad, rs_feat, rs_grad, rs_f, rs_b, ready,
):
    s = lax.axis_index("section")
    q = lax.axis_index("seq")
    c = lax.axis_index("head")
    y = q // 4
    x = lax.rem(q, 4)
    co = x // 2
    half = lax.rem(x, 2)
    first_head = 32 * half + 16 * c
    R_SEG, R_STEP, R_DEC, R_MAP, R_PREV, R_GF, R_GS, R_GD, R_PM, R_RD, R_A, R_B, R_C, R_CROSS, R_SUM = range(15)

    barrier = pltpu.get_barrier_semaphore()
    load_seg = pltpu.make_async_copy(seg, SEGI, rs_one.at[R_A])
    load_in = pltpu.make_async_copy(map_in, RAW.at[0], rs_one.at[R_B])
    load_out = pltpu.make_async_copy(map_out, RAW.at[1], rs_one.at[R_C])
    load_seg.start()
    load_in.start()
    load_out.start()

    def greet(target):
        pl.semaphore_signal(barrier, inc=1, device_id=target, device_id_type=MESH)

    for dx in range(1, 4):
        greet(place(s, y, x + dx, 0))

    @pl.when(c == 1)
    def _():
        greet(place(s, y, x, 0))

    for dx in range(4):
        greet(place(s + 1, y, x + dx, 1))
    for dy in range(1, 4):
        greet(place(s, y + dy, x, 1))

    load_seg.wait()
    SEGF[...] = jnp.broadcast_to(SEGI[...].astype(F32), (8, T))
    load_in.wait()
    load_out.wait()
    for g in range(2):
        MAPS[g, 0] = RAW[0, :, g, :]
        MAPS[g, 1] = RAW[1, :, g, :]

    @pl.when(c == 0)
    def _():
        pl.semaphore_wait(barrier, 7)
        pl.semaphore_signal(ready, inc=1, device_id=place(s, y, x, 1), device_id_type=MESH)

    @pl.when(c == 1)
    def _():
        pl.semaphore_wait(ready, 1)

    pending = []
    count = itertools.count()

    def send(src, dst, rsem, target, own=None):
        copy = pltpu.make_async_remote_copy(
            src_ref=src, dst_ref=dst, send_sem=ssem.at[next(count)], recv_sem=rsem,
            device_id=target, device_id_type=MESH,
        )
        if own is None:
            copy.start()
            pending.append((None, copy))
        else:
            away = jnp.logical_not(own)

            @pl.when(own)
            def _():
                pltpu.make_async_copy(src, dst, rsem).start()

            @pl.when(away)
            def _():
                copy.start()

            pending.append((away, copy))

    def sent(sends):
        for away, copy in sends:
            if away is None:
                copy.wait_send()
            else:
                @pl.when(away)
                def _(copy=copy):
                    copy.wait_send()

    def arrived(ref, sem):
        pltpu.make_async_copy(ref, ref, sem).wait()

    pltpu.make_async_copy(SEGF, SEG.at[x], rs_one.at[R_SEG]).start()
    for dx in range(1, 4):
        send(SEGF, SEG.at[x], rs_one.at[R_SEG], place(s, y, x + dx, c))
    chips = [lax.rem(x + dx, 4) for dx in range(4)]
    workers = []
    for gl in range(2):
        for dc in range(2):
            xw = 2 * c + gl
            own = (xw == x) if dc == 0 else None
            workers.append((gl, xw, lax.rem(c + dc, 2), own))

    def to_owner(src, dst, rsem, dx):
        own = (c == co) if dx == 0 else None
        send(src, dst, rsem, place(s, y, chips[dx], co), own)

    for gl, xw, cw, own in workers:
        rows = pl.ds(pl.multiple_of(32 * gl + 16 * cw, 16), 16)
        send(step.at[rows], STEP.at[x], rs_one.at[R_STEP], place(s, y, xw, cw), own)
        send(dec.at[rows], DEC.at[x], rs_one.at[R_DEC], place(s, y, xw, cw), own)
    for gl, xw, cw, own in workers:
        send(MAPS.at[gl, cw], MAP.at[cw, x], rs_one.at[R_MAP], place(s, y, xw, cw), own)
    feat_sends = {}

    def issue_feat(k):
        before = len(pending)
        for gl, xw, cw, own in workers:
            rows = pl.ds(pl.multiple_of((32 * gl + 16 * cw + HC * k) * W, CW), CW)
            send(feat.at[rows], XT.at[k, x], rs_feat.at[k], place(s, y, xw, cw), own)
        feat_sends[k] = pending[before:]
        del pending[before:]

    def issue_grad(k):
        for dx in range(4):
            for dc in range(2):
                xw = lax.rem(x + dx, 4)
                cw = lax.rem(c + dc, 2)
                cols = pl.ds(pl.multiple_of((32 * xw + 16 * cw + HC * k) * W, CW), CW)
                pltpu.make_async_remote_copy(
                    src_ref=grad.at[:, cols],
                    dst_ref=GRN.at[k, x, pl.ds(pl.multiple_of(64 * c, 64), 64), :],
                    send_sem=ss_grad.at[k],
                    recv_sem=rs_grad.at[k],
                    device_id=place(s - 1, y, xw, cw),
                    device_id_type=MESH,
                ).start()

    def gone(k):
        sent(feat_sends[k])
        arrived(grad.at[:, pl.ds(0, 8 * CW)], ss_grad.at[k])

    for k in range(WINDOW):
        issue_feat(k)

    @pl.when(c == 1)
    def _():
        pl.semaphore_wait(barrier, 14)
        pl.semaphore_signal(ready, inc=1, device_id=place(s, y, x, 0), device_id_type=MESH)

    @pl.when(c == 0)
    def _():
        pl.semaphore_wait(ready, 1)

    for k in range(WINDOW):
        issue_grad(k)

    arrived(SEG, rs_one.at[R_SEG])
    send(SEG.at[3], PREV, rs_one.at[R_PREV], place(s, y + 1, x, c))
    arrived(STEP, rs_one.at[R_STEP])
    arrived(DEC, rs_one.at[R_DEC])
    row_id = lax.broadcasted_iota(jnp.int32, (T, T), 0)
    col_id = lax.broadcasted_iota(jnp.int32, (T, T), 1)
    upper = (row_id <= col_id).astype(F32)
    for b in range(ROW):
        total = dot(DEC[b], upper, HIGHEST)
        L[b] = total
        padded = jnp.concatenate([total, jnp.zeros((T - HEADS, T), F32)], axis=0)
        LT[b] = jnp.transpose(padded)
        seg_row = SEG[b][0:1, :]
        seg_col = jnp.transpose(jnp.broadcast_to(seg_row, (T, T)))
        same = (seg_col == seg_row).astype(F32)
        MASK[b] = jnp.where(row_id >= col_id, same, 0.0)
        PRE[b] = jnp.where(row_id < col_id, same, 0.0)
    arrived(PREV, rs_one.at[R_PREV])
    first = (y > 0).astype(F32)
    decays = []
    for b in range(ROW):
        total = L[b]
        seg_row = SEG[b][0:1, :]
        if b == 0:
            previous = PREV[0:1, T - 1 : T] * first
        else:
            previous = SEG[b - 1][0:1, T - 1 : T]
        last = total[:, T - 1 : T]
        seg_last = seg_row[:, T - 1 : T]
        carried = (seg_row == previous).astype(F32)
        tail = (seg_row == seg_last).astype(F32)
        HW[b] = carried * jnp.exp(total)
        tw = tail * jnp.exp(last - total)
        TW[b] = tw
        STW[b] = STEP[b] * tw
        d = jnp.broadcast_to((seg_last == previous).astype(F32) * jnp.exp(last), (HEADS, N))
        DB[b] = d
        decays.append(d)
    one = jnp.ones((HEADS, N), F32)
    run = one
    for b in range(ROW):
        CF[b] = run
        run = run * decays[b]
    CF[ROW] = run
    run = one
    for b in reversed(range(ROW)):
        CB[b] = run
        run = run * decays[b]
    ROWD[...] = CF[ROW][:, 0:T]
    pltpu.make_async_copy(ROWD, RDEC.at[y], rs_one.at[R_RD]).start()
    for dy in range(1, 4):
        send(ROWD, RDEC.at[y], rs_one.at[R_RD], place(s, y + dy, x, c))
    arrived(MAP.at[c], rs_one.at[R_MAP])
    send(MAP.at[c], MAP.at[c], rs_one.at[R_CROSS], place(s, y, x, c + 1))
    arrived(MAP.at[1 - c], rs_one.at[R_CROSS])
    for b in range(ROW):
        MAPT[b, 0] = jnp.transpose(MAP[0, b])
        MAPT[b, 1] = jnp.transpose(MAP[1, b])
        CM[b] = dot(MAP[1, b], MAPT[b, 0])
        WS[b] = jnp.zeros((T, T), F32)
        RK[b] = jnp.zeros((T, T), F32)
        GIM[b] = jnp.zeros((T, N), F32)
        GOM[b] = jnp.zeros((T, N), F32)

    def by_head(a):
        return a.reshape(HC, W, a.shape[-1])

    def scaled(a, w):
        return (by_head(a) * w[:, None, :]).reshape(a.shape)

    def heads_of(ref, b, k):
        return ref[b, HC * k : HC * (k + 1), :]

    def copy_f(k, to):
        return pltpu.make_async_remote_copy(
            src_ref=ES.at[k], dst_ref=RF.at[k, y], send_sem=ssem.at[FBASE + 6 * k + to - 1],
            recv_sem=rs_f.at[k, y], device_id=place(s, to, x, c), device_id_type=MESH,
        )

    def copy_b(k, to):
        return pltpu.make_async_remote_copy(
            src_ref=GS.at[k], dst_ref=RB.at[k, y - 1], send_sem=ssem.at[FBASE + 6 * k + 3 + to],
            recv_sem=rs_b.at[k, y - 1], device_id=place(s, to, x, c), device_id_type=MESH,
        )

    def local_states(k):
        arrived(XT.at[k], rs_feat.at[k])
        total = jnp.zeros((CW, N), F32)
        PF[k, 0] = total
        for b in range(ROW):
            xw = scaled(XT[k, b].astype(F32), heads_of(STW, b, k)).astype(BF16)
            XW[k, b] = xw
            total = scaled(total, heads_of(DB, b, k)) + dot(xw, MAP[0, b])
            PF[k, b + 1] = total
        ES[k] = total.astype(BF16)
        for to in range(1, 4):
            @pl.when(y < to)
            def _(to=to):
                copy_f(k, to).start()

    def local_grads(k):
        arrived(GRN.at[k], rs_grad.at[k])
        total = jnp.zeros((CW, N), F32)
        PB[k, ROW] = total
        for b in reversed(range(ROW)):
            gt = jnp.transpose(GRN[k, b])
            GRT[k, b] = gt
            gh = scaled(gt.astype(F32), heads_of(HW, b, k)).astype(BF16)
            GHW[k, b] = gh
            total = scaled(total, heads_of(DB, b, k)) + dot(gh, MAP[1, b])
            PB[k, b] = total
        GS[k] = total.astype(BF16)
        for to in range(3):
            @pl.when(y > to)
            def _(to=to):
                copy_b(k, to).start()

    def enter_f(k):
        EA[...] = jnp.zeros((CW, N), F32)
        for src in range(3):
            @pl.when(y > src)
            def _(src=src):
                arrived(RF.at[k, src], rs_f.at[k, src])
                coef = COF[src, HC * k : HC * (k + 1), :]
                EA[...] += scaled(RF[k, src].astype(F32), coef)

    def enter_b(k):
        GA[...] = jnp.zeros((CW, N), F32)
        for src in range(1, 4):
            @pl.when(y < src)
            def _(src=src):
                arrived(RB.at[k, src - 1], rs_b.at[k, src - 1])
                coef = COB[src - 1, HC * k : HC * (k + 1), :]
                GA[...] += scaled(RB[k, src - 1].astype(F32), coef)

    def intra(k):
        def one_block(b, carry):
            xt = XT[k, b]
            zero = jnp.zeros((W, T), BF16)
            spread = jnp.concatenate(
                [
                    jnp.concatenate(
                        [xt[W * h : W * (h + 1)] if h == j else zero for j in range(HC)], axis=1
                    )
                    for h in range(HC)
                ],
                axis=0,
            )
            pairs = dot(GRN[k, b], spread)
            mask = MASK[b] > 0.0
            cross = CM[b]
            columns = LT[b]
            held = WS[b]
            sums = RK[b]
            lane = lax.broadcasted_iota(jnp.int32, (T, T), 1)
            cols = []
            for h in range(HC):
                head = HC * k + h
                gap = columns[:, head : head + 1] - L[b, head : head + 1, :]
                m = jnp.where(mask, jnp.exp(gap), 0.0)
                a = (m * cross).astype(BF16)
                VI[k, b, W * h : W * (h + 1), :] = dot(GRT[k, b, W * h : W * (h + 1), :], a)
                wh = m * pairs[:, T * h : T * (h + 1)] * STEP[b, head : head + 1, :]
                held = held + wh
                kk = wh * cross
                cols.append(jnp.sum(kk, axis=0, keepdims=True))
                sums = jnp.where(lane == head, jnp.sum(kk, axis=1, keepdims=True), sums)
            CK[b, HC * k : HC * (k + 1), :] = jnp.concatenate(cols, axis=0)
            WS[b] = held
            RK[b] = sums
            return carry

        lax.fori_loop(0, ROW, one_block, 0, unroll=4)

    def row_factors():
        arrived(RDEC, rs_one.at[R_RD])
        one = jnp.ones((HEADS, T), F32)
        for src in range(3):
            coef = one
            for r in range(src + 1, 3):
                coef = coef * jnp.where(y > r, RDEC[r], one)
            COF[src] = jnp.concatenate([coef, coef], axis=1)
            coef = one
            for r in range(1, src + 1):
                coef = coef * jnp.where(y < r, RDEC[r], one)
            COB[src] = jnp.concatenate([coef, coef], axis=1)

    def finish_f(k):
        enter_f(k)

        def one_block(b, carry):
            eb = (PF[k, b] + scaled(EA[...], heads_of(CF, b, k))).astype(BF16)
            EB[k, b] = eb
            seen = dot(eb, MAPT[b, 1])
            hs = slice(HC * k, HC * (k + 1))
            U[b, hs, :] = heads_of(HW, b, k) * jnp.sum(by_head(GRT[k, b].astype(F32) * seen), axis=1)
            GOM[b] += dot_tn(GHW[k, b], eb)
            return carry

        lax.fori_loop(0, ROW, one_block, 0, unroll=4)

    def finish_b(k):
        enter_b(k)

        def one_block(b, carry):
            gb = (PB[k, b + 1] + scaled(GA[...], heads_of(CB, b, k))).astype(BF16)
            lift = dot(gb, MAPT[b, 0])
            val = VI[k, b] + scaled(lift, heads_of(TW, b, k))
            GF[k, b] = scaled(val, heads_of(STEP, b, k)).astype(BF16)
            hs = slice(HC * k, HC * (k + 1))
            V[b, hs, :] = heads_of(STW, b, k) * jnp.sum(by_head(XT[k, b].astype(F32) * lift), axis=1)
            both = jnp.sum(by_head(EB[k, b].astype(F32) * gb.astype(F32)), axis=1)
            B4[b, hs, :] = jnp.broadcast_to(jnp.sum(both, axis=1, keepdims=True), (HC, T))
            GIM[b] += dot_tn(XW[k, b], gb)
            return carry

        lax.fori_loop(0, ROW, one_block, 0, unroll=4)
        for dx in range(4):
            rows = pl.ds(pl.multiple_of((first_head + HC * k) * W, CW), CW)
            to_owner(GF.at[k, chips[dx]], gf_out.at[rows], rs_one.at[R_GF], dx)

    def part_of_map(m, total):
        @pl.when(c != m)
        def _():
            for b in range(ROW):
                PMS[b] = total[b].astype(BF16)
            cross[m].start()

    def sum_of_map(m, total):
        @pl.when(c == m)
        def _():
            arrived(PX, rs_one.at[R_SUM])
            for b in range(ROW):
                PO[b] = (total[b] + PX[b].astype(F32)).astype(BF16)
            for dx in range(4):
                if dx == 0:
                    @pl.when(c == co)
                    def _():
                        pltpu.make_async_copy(PO.at[x], PM.at[half, m], rs_one.at[R_PM]).start()

                    @pl.when(c != co)
                    def _():
                        summed[m][0].start()
                else:
                    summed[m][dx].start()

    cross, summed = [], []
    for m in range(2):
        cross.append(
            pltpu.make_async_remote_copy(
                src_ref=PMS, dst_ref=PX, send_sem=ssem.at[next(count)], recv_sem=rs_one.at[R_SUM],
                device_id=place(s, y, x, c + 1), device_id_type=MESH,
            )
        )
        pending.append((c != m, cross[m]))
        summed.append([])
        for dx in range(4):
            summed[m].append(
                pltpu.make_async_remote_copy(
                    src_ref=PO.at[chips[dx]], dst_ref=PM.at[half, m], send_sem=ssem.at[next(count)],
                    recv_sem=rs_one.at[R_PM], device_id=place(s, y, chips[dx], co),
                    device_id_type=MESH,
                )
            )
            going = c == m
            if dx == 0:
                going = jnp.logical_and(going, c != co)
            pending.append((going, summed[m][dx]))

    for k in range(CHUNKS):
        local_states(k)
        local_grads(k)
        gone(k)
        if k + WINDOW < CHUNKS:
            issue_feat(k + WINDOW)
            issue_grad(k + WINDOW)
        intra(k)
        if k == 0:
            row_factors()
        if k + 1 == CHUNKS:
            for b in range(ROW):
                w = WS[b].astype(BF16)
                GOM[b] += dot(w, MAP[0, b])
                GIM[b] += dot_tn(w, MAP[1, b])
        if k >= LAG:
            finish_f(k - LAG)
            finish_b(k - LAG)
    for k in range(CHUNKS - LAG, CHUNKS):
        finish_f(k)
        if k + 1 == CHUNKS:
            part_of_map(1, GOM)
            for b in range(ROW):
                row_sums = jnp.transpose(RK[b])[0:HEADS, :]
                GDS[b] = dot(row_sums - CK[b] + U[b], MASK[b], HIGHEST)
        finish_b(k)
    part_of_map(0, GIM)
    sum_of_map(1, GOM)

    for b in range(ROW):
        v = V[b]
        GSS[b] = (CK[b] + v) / STEP[b]
        GDS[b] += dot(v, PRE[b], HIGHEST) + HW[b] * TW[b] * B4[b]
    for dx in range(4):
        rows = pl.ds(pl.multiple_of(first_head, 16), 16)
        to_owner(GSS.at[chips[dx]], gs_out.at[rows], rs_one.at[R_GS], dx)
        to_owner(GDS.at[chips[dx]], gd_out.at[rows], rs_one.at[R_GD], dx)

    sum_of_map(0, GIM)
    arrived(PM, rs_one.at[R_PM])
    arrived(gf_out, rs_one.at[R_GF])
    arrived(gs_out, rs_one.at[R_GS])
    arrived(gd_out, rs_one.at[R_GD])
    assert next(count) <= FBASE
    sent(pending)
    for k in range(CHUNKS):
        for to in range(1, 4):
            @pl.when(y < to)
            def _():
                copy_f(k, to).wait_send()
        for to in range(3):
            @pl.when(y > to)
            def _():
                copy_b(k, to).wait_send()


def settle(
    gf, gs, gd, pm, gf_out, gs_out, gd_out, gim_out, gom_out,
    held, steps, maps, sums, sem_in, sem_out,
):
    size = 64 * W // PIECES
    reads, writes = [], []
    for g in range(2):
        reads.append(pltpu.make_async_copy(pm.at[g], maps.at[g], sem_in.at[g]))
    for i in range(PIECES):
        rows = pl.ds(i * size, size)
        reads.append(pltpu.make_async_copy(gf.at[rows], held.at[rows], sem_in.at[2 + i]))
        writes.append(pltpu.make_async_copy(held.at[rows], gf_out.at[rows], sem_out.at[i]))
    for i, (a, b) in enumerate(((gs, gs_out), (gd, gd_out))):
        reads.append(pltpu.make_async_copy(a, steps.at[i], sem_in.at[2 + PIECES + i]))
        writes.append(pltpu.make_async_copy(steps.at[i], b, sem_out.at[PIECES + i]))
    for copy in reads:
        copy.start()
    for g in range(2):
        reads[g].wait()
        for m in range(2):
            sums[m, :, g, :] = maps[g, m].astype(F32)
    for m, out in enumerate((gim_out, gom_out)):
        copy = pltpu.make_async_copy(sums.at[m], out, sem_out.at[PIECES + 2 + m])
        copy.start()
        writes.append(copy)
    for i in range(PIECES + 2):
        reads[2 + i].wait()
        writes[i].start()
    for copy in writes:
        copy.wait()


def per_device(features, step_size, log_decay, input_map, output_map, segment, sent_grad):
    feat = jnp.transpose(features[0], (1, 2, 0)).reshape(64 * W, T)
    step = step_size[0].T
    dec = log_decay[0].T
    grad = sent_grad[0]
    any_ = pl.BlockSpec(memory_space=pltpu.HBM)
    V_ = pltpu.VMEM
    scratch = [
        V_((CHUNKS, ROW, CW, T), BF16),
        V_((CHUNKS, ROW, CW, T), BF16),
        V_((CHUNKS, ROW, T, CW), BF16),
        V_((CHUNKS, ROW, CW, T), BF16),
        V_((CHUNKS, ROW, CW, T), BF16),
        V_((2, ROW, T, N), BF16),
        V_((ROW, HEADS, T), F32),
        V_((ROW, HEADS, T), F32),
        V_((ROW, 8, T), F32),
        V_((8, T), F32),
        V_((ROW, HEADS, T), F32),
        V_((ROW, T, T), F32),
        V_((ROW, HEADS, T), F32),
        V_((ROW, HEADS, T), F32),
        V_((ROW, HEADS, T), F32),
        V_((ROW, HEADS, N), F32),
        V_((ROW + 1, HEADS, N), F32),
        V_((ROW, HEADS, N), F32),
        V_((ROW, T, T), F32),
        V_((ROW, T, T), F32),
        V_((ROW, T, T), F32),
        V_((CHUNKS, ROW + 1, CW, N), F32),
        V_((CHUNKS, ROW + 1, CW, N), F32),
        V_((CHUNKS, ROW, CW, T), F32),
        V_((ROW, T, T), F32),
        V_((ROW, HEADS, T), F32),
        V_((ROW, T, T), F32),
        V_((ROW, HEADS, T), F32),
        V_((ROW, HEADS, T), F32),
        V_((ROW, HEADS, T), F32),
        V_((CHUNKS, 3, CW, N), BF16),
        V_((CHUNKS, 3, CW, N), BF16),
        V_((CHUNKS, CW, N), BF16),
        V_((CHUNKS, CW, N), BF16),
        V_((CW, N), F32),
        V_((CW, N), F32),
        V_((CHUNKS, ROW, CW, N), BF16),
        V_((3, HEADS, N), F32),
        V_((3, HEADS, N), F32),
        V_((4, HEADS, T), F32),
        V_((HEADS, T), F32),
        V_((ROW, T, N), F32),
        V_((ROW, T, N), F32),
        V_((ROW, T, N), BF16),
        V_((ROW, T, N), BF16),
        V_((ROW, T, N), BF16),
        V_((CHUNKS, ROW, CW, T), BF16),
        V_((ROW, HEADS, T), F32),
        V_((ROW, HEADS, T), F32),
        V_((1, T), jnp.int32),
        V_((8, T), F32),
        V_((2, T, 2, N), BF16),
        V_((2, 2, T, N), BF16),
        V_((ROW, 2, N, T), BF16),
        pltpu.SemaphoreType.DMA((FBASE + 6 * CHUNKS,)),
        pltpu.SemaphoreType.DMA((15,)),
        pltpu.SemaphoreType.DMA((CHUNKS,)),
        pltpu.SemaphoreType.DMA((CHUNKS,)),
        pltpu.SemaphoreType.DMA((CHUNKS,)),
        pltpu.SemaphoreType.DMA((CHUNKS, 3)),
        pltpu.SemaphoreType.DMA((CHUNKS, 3)),
        pltpu.SemaphoreType.REGULAR,
    ]
    gf, gs, gd, pm = pl.pallas_call(
        kernel,
        out_shape=(
            jax.ShapeDtypeStruct((64 * W, T), BF16),
            jax.ShapeDtypeStruct((64, T), F32),
            jax.ShapeDtypeStruct((64, T), F32),
            jax.ShapeDtypeStruct((2, 2, T, N), BF16),
        ),
        in_specs=[any_] * 7,
        out_specs=(any_, any_, any_, any_),
        scratch_shapes=scratch,
        compiler_params=pltpu.CompilerParams(
            collective_id=0, has_side_effects=True, vmem_limit_bytes=60 * 2**20
        ),
        name="ssd_backward",
    )(feat, step, dec, input_map[0], output_map[0], segment, grad)
    gf, gs, gd, gim, gom = pl.pallas_call(
        settle,
        out_shape=(
            jax.ShapeDtypeStruct((64 * W, T), BF16),
            jax.ShapeDtypeStruct((64, T), F32),
            jax.ShapeDtypeStruct((64, T), F32),
            jax.ShapeDtypeStruct((T, 2, N), F32),
            jax.ShapeDtypeStruct((T, 2, N), F32),
        ),
        in_specs=[any_] * 4,
        out_specs=(any_,) * 5,
        scratch_shapes=[
            V_((64 * W, T), BF16),
            V_((2, 64, T), F32),
            V_((2, 2, T, N), BF16),
            V_((2, T, 2, N), F32),
            pltpu.SemaphoreType.DMA((PIECES + 4,)),
            pltpu.SemaphoreType.DMA((PIECES + 4,)),
        ],
        compiler_params=pltpu.CompilerParams(vmem_limit_bytes=60 * 2**20),
        name="settle",
    )(gf, gs, gd, pm)
    return (
        jnp.transpose(gf.reshape(64, W, T), (2, 0, 1))[None],
        gs.T[None],
        gd.T[None],
        gim[None],
        gom[None],
    )


def solution(mesh):
    placed = (
        P("section", "seq", "head", None),
        P("section", "seq", "head"),
        P("section", "seq", "head"),
        P("section", "seq", "head", None),
        P("section", "seq", "head", None),
        P("section", "seq"),
        P("section", ("seq", "head"), None),
    )
    return jax.shard_map(
        per_device,
        mesh=mesh,
        in_specs=placed,
        out_specs=(
            P("section", "seq", "head", None),
            P("section", "seq", "head"),
            P("section", "seq", "head"),
            P("section", "seq", "head", None),
            P("section", "seq", "head", None),
        ),
        check_vma=False,
    )
```
